32 devices in a mesh: dp: 4 (over y, x), expert: 8 (over z, core).
Axes of the slice: x: 2, y: 2, z: 4, core: 2. Of those that a mesh axis runs over, the one named last changes fastest.
Arguments:
- tokens: bfloat16 [4096, 2048], P(('dp', 'expert')), may hold values from -6 to 6
- initial_expert_index: int32 [4096, 4], P(('dp', 'expert')), may hold values from 0 to 15, all different within a row; in each aligned block of 128 rows (0 to 127, 128 to 255, ...) at most 36 rows name the same one
- pruned_expert_index: int32 [4096, 4], P(('dp', 'expert')), may hold values from 0 to 7, all different within a row; in each aligned block of 128 rows (0 to 127, 128 to 255, ...) at most 72 rows name the same one
- initial_router_scores: float32 [4096, 4], P(('dp', 'expert')), may hold values from 0.05 to 1
- pruned_router_scores: float32 [4096, 4], P(('dp', 'expert')), may hold values from 0.05 to 1
- gate_weight: bfloat16 [16, 2048, 768], P('expert', 'dp'), may hold values from -0.125 to 0.125
- up_weight: bfloat16 [16, 2048, 768], P('expert', 'dp'), may hold values from -0.125 to 0.125
- down_weight: bfloat16 [16, 768, 2048], P('expert', None, 'dp'), may hold values from -0.21875 to 0.21875
- adapter_first_weight: float32 [8, 768, 64], P('expert'), may hold values from -0.21875 to 0.21875
- adapter_second_weight: float32 [8, 64, 2048], P('expert'), may hold values from -0.75 to 0.75
Outputs:
- grad_a: float32 [8, 768, 64], P('expert', 'dp')
- grad_b: float32 [8, 64, 2048], P('expert', None, 'dp')
The draws below stay inside these ranges and needn't reach their ends.
Inputs may be any that keep to these rules, and one draw needn't show every extreme that they name: `initial_expert_index`: the 4 entries of a row differ. In each aligned block of 128 rows no expert is named more than 36 times, a bound that some block reaches. `pruned_expert_index`: the 4 entries of a row differ. In each aligned block of 128 rows no expert is named more than 72 times, a bound that some block reaches.
All inputs are finite; a program needn't handle non-finite values.
Results may differ from the reference program's by a relative error of at most 0.0029.
Values may be sent and summed in bfloat16 or wider, within the bound.
No kernel may reach another device: no remote copies, remote signals or barrier semaphores. Data moves between devices by JAX's collectives and lax.ppermute only.
A program may use at most 128 MiB of HBM per device.

```python
import math
import jax
import jax.numpy as jnp
import numpy as np
from jax import lax

MODEL_WIDTH = 2048
EXPERT_HIDDEN = 768
ADAPTER_RANK = 64
TOPK = 4
TOK_DEV = 128
TOKENS = 4096
EXPERTS = 16
PRUNED_EXPERTS = 8
CAP_O = 36
CAP_P = 72


def level_of(key, dims, cuts, least, largest):
    def one(dim, shards_of):
        draws = jax.random.uniform(jax.random.fold_in(jax.random.fold_in(key, 6), dim), (shards_of,), jnp.float32, least / len(cuts), largest / len(cuts))
        return jnp.repeat(jnp.exp(draws), dims[dim] // shards_of).reshape((-1,) + (1,) * (len(dims) - dim - 1))

    level = one(*cuts[0])
    for cut in cuts[1:]:
        level = level * one(*cut)
    return level


def assign_block(key, own, number, rows, count, top, reach, skew):
    sequence = jax.random.permutation(key, count)
    heavy_load, common = load_shares(count, rows * top, reach, skew, True), load_shares(count, rows * top, reach, skew, False)
    places = jnp.arange(count)

    def named(tallies, turn):
        used = int((tallies > 0).sum())
        fixed = max(1, used // 4)
        moved = fixed + (places - fixed + turn * (used - fixed)) % max(1, count - fixed)
        return jnp.zeros((count,), jnp.int32).at[sequence[jnp.where(places < fixed, places, moved)]].set(jnp.asarray(tallies, jnp.int32))

    tallies = jnp.where(number % 4 == 0, named(heavy_load, number // 4), named(common, number - number // 4 - 1))
    mixed = jax.random.permutation(jax.random.fold_in(own, 3), count)
    source_of, receiver = mixed[0:count // 2 * 2:2], mixed[1:count // 2 * 2:2]
    slack = jnp.minimum(tallies[source_of] - 1, reach - tallies[receiver]) // 2
    slack = jnp.where((source_of == sequence[0]) | (receiver == sequence[0]) | (tallies[receiver] == 0), 0, jnp.maximum(slack, 0))
    moved = jax.random.randint(jax.random.fold_in(own, 4), (count // 2,), 0, 1 << 20) % (slack + 1)
    tallies = tallies.at[source_of].add(-moved).at[receiver].add(moved)
    members = jnp.searchsorted(jnp.cumsum(tallies), jnp.arange(rows * top), side="right").astype(jnp.int32)
    table = members.reshape(top, rows).T
    table = table[jax.random.permutation(jax.random.fold_in(own, 1), rows)]
    turn = jax.random.randint(jax.random.fold_in(own, 2), (rows, 1), 0, top)
    return jnp.take_along_axis(table, (jnp.arange(top)[None, :] + turn) % top, axis=1)


def load_shares(number_of, total, limit, slope, full):
    portions = [(1 << 20) // math.isqrt(standing ** slope) + 1 for standing in range(1, number_of + 1)]
    largest = limit if full else min(limit, max(-(-total // number_of), total * portions[0] // sum(portions)))
    least = 1 if total - largest >= number_of - 1 else 0
    holding, rest = [largest] + [least] * (number_of - 1), total - largest - least * (number_of - 1)
    while rest > 0:
        candidates = [i for i in range(1, number_of) if holding[i] < largest] or [i for i in range(1, number_of) if holding[i] < limit]
        mass, budget = sum([portions[i] for i in candidates]), rest
        for i in candidates:
            extra = min(limit - holding[i], max(1, budget * portions[i] // mass), rest)
            holding[i] = holding[i] + extra
            rest = rest - extra
    return np.array(holding)


def normal_values(stream_key, dims, width, most, pieces=(), held_as=jnp.bfloat16):
    array = jax.random.normal(stream_key, dims, jnp.float32) * width
    if len(pieces) > 0:
        array = level_of(stream_key, dims, pieces, -0.22, 0.18) * array
    return jnp.clip(array, min=-most, max=most).astype(held_as)


def setup_inputs(seed: int = 0) -> dict:
    splits = jax.random.split(jax.random.key(seed), 11)
    tokens = normal_values(splits[0], (TOKENS, MODEL_WIDTH), 1.0, 6.0, ((0, 32),))
    initial_expert_index_keys = jax.random.split(jax.random.fold_in(splits[1], 1), TOKENS // TOK_DEV)
    initial_expert_index_turns = jax.random.permutation(jax.random.fold_in(splits[1], 3), TOKENS // TOK_DEV)
    initial_expert_index = jax.vmap(lambda own, number: assign_block(jax.random.fold_in(splits[1], 2), own, number, TOK_DEV, EXPERTS, TOPK, CAP_O, 1))(initial_expert_index_keys, initial_expert_index_turns).reshape((TOKENS, TOPK))
    pruned_expert_index_keys = jax.random.split(jax.random.fold_in(splits[2], 1), TOKENS // TOK_DEV)
    pruned_expert_index_turns = jax.random.permutation(jax.random.fold_in(splits[2], 3), TOKENS // TOK_DEV)
    pruned_expert_index = jax.vmap(lambda own, number: assign_block(jax.random.fold_in(splits[2], 2), own, number, TOK_DEV, PRUNED_EXPERTS, TOPK, CAP_P, 1))(pruned_expert_index_keys, pruned_expert_index_turns).reshape((TOKENS, TOPK))
    initial_router_scores = jnp.clip(0.05 + 0.95 * jax.random.uniform(splits[3], (TOKENS, TOPK), jnp.float32) ** level_of(splits[3], (TOKENS, TOPK), ((0, 32),), -0.2, 0.2), 0.05, 1.0)
    pruned_router_scores = jnp.clip(0.05 + 0.95 * jax.random.uniform(splits[4], (TOKENS, TOPK), jnp.float32) ** level_of(splits[4], (TOKENS, TOPK), ((0, 32),), -0.2, 0.2), 0.05, 1.0)
    gate_weight = normal_values(splits[5], (EXPERTS, MODEL_WIDTH, EXPERT_HIDDEN), MODEL_WIDTH ** -0.5, 0.125, ((0, 8), (1, 4)))
    up_weight = normal_values(splits[6], (EXPERTS, MODEL_WIDTH, EXPERT_HIDDEN), MODEL_WIDTH ** -0.5, 0.125, ((0, 8), (1, 4)))
    down_weight = normal_values(splits[7], (EXPERTS, EXPERT_HIDDEN, MODEL_WIDTH), EXPERT_HIDDEN ** -0.5, 0.21875, ((0, 8), (2, 4)))
    adapter_first_weight = normal_values(splits[8], (PRUNED_EXPERTS, EXPERT_HIDDEN, ADAPTER_RANK), EXPERT_HIDDEN ** -0.5, 0.21875, ((0, 8),), jnp.float32)
    adapter_second_weight = normal_values(splits[9], (PRUNED_EXPERTS, ADAPTER_RANK, MODEL_WIDTH), ADAPTER_RANK ** -0.5, 0.75, ((0, 8),), jnp.float32)
    return dict(tokens=tokens, initial_expert_index=initial_expert_index, pruned_expert_index=pruned_expert_index, initial_router_scores=initial_router_scores, pruned_router_scores=pruned_router_scores, gate_weight=gate_weight, up_weight=up_weight, down_weight=down_weight, adapter_first_weight=adapter_first_weight, adapter_second_weight=adapter_second_weight)


def route_tables(route_ids, weight, num_experts, capacity):
    blocks = route_ids.shape[0] // TOK_DEV
    shares = weight / jnp.sum(weight, axis=1, keepdims=True)
    flat_ids = route_ids.reshape(blocks, TOK_DEV * TOPK)
    hit_table = (flat_ids[:, :, None] == jnp.arange(num_experts, dtype=jnp.int32)[None, None, :]).astype(jnp.int32)
    slot_index = jnp.sum(hit_table * (jnp.cumsum(hit_table, axis=1) - 1), axis=2)
    block_base = (jnp.arange(blocks, dtype=jnp.int32) * (num_experts * capacity))[:, None]
    dest_index = (block_base + flat_ids * capacity + slot_index).reshape(-1)
    owner_token = ((jnp.arange(blocks, dtype=jnp.int32) * TOK_DEV)[:, None] + jnp.arange(TOK_DEV * TOPK, dtype=jnp.int32)[None, :] // TOPK).reshape(-1)
    slot_token = jnp.zeros(blocks * num_experts * capacity, jnp.int32).at[dest_index].set(owner_token)
    slot_weight = jnp.zeros(blocks * num_experts * capacity, jnp.float32).at[dest_index].set(shares.reshape(-1))
    slot_token = slot_token.reshape(blocks, num_experts, capacity).transpose(1, 0, 2).reshape(num_experts, -1)
    slot_weight = slot_weight.reshape(blocks, num_experts, capacity).transpose(1, 0, 2).reshape(num_experts, -1)
    return slot_token, slot_weight


def hidden_rows(rows, gate_mat, up_mat):
    gate_part = jnp.dot(rows, gate_mat, preferred_element_type=jnp.float32)
    up_part = jnp.dot(rows, up_mat, preferred_element_type=jnp.float32)
    return (jax.nn.silu(gate_part) * up_part).astype(jnp.bfloat16)


def reference(tokens, initial_expert_index, pruned_expert_index, initial_router_scores, pruned_router_scores, gate_weight, up_weight, down_weight, adapter_first_weight, adapter_second_weight):
    frozen_tok, frozen_wts = route_tables(initial_expert_index, initial_router_scores, EXPERTS, CAP_O)
    pruned_token_rows, pruned_gate_weights = route_tables(pruned_expert_index, pruned_router_scores, PRUNED_EXPERTS, CAP_P)
    offset_index = jnp.zeros(tokens.shape, jnp.float32)

    def frozen_step(total, inputs):
        tok_index, tok_share, gate_mat, up_mat, down_mat = inputs
        rows = jnp.take(tokens, tok_index, axis=0)
        hidden = hidden_rows(rows, gate_mat, up_mat)
        frozen_row = jnp.dot(hidden, down_mat, preferred_element_type=jnp.float32).astype(jnp.bfloat16)
        return total.at[tok_index].add(frozen_row.astype(jnp.float32) * tok_share[:, None]), None

    target, discarded_value = lax.scan(frozen_step, offset_index, (frozen_tok, frozen_wts, gate_weight, up_weight, down_weight))

    def pruned_update(total, inputs):
        tok_index, tok_share, gate_mat, up_mat, down_mat, first_factor, second_factor = inputs
        rows = jnp.take(tokens, tok_index, axis=0)
        hidden = hidden_rows(rows, gate_mat, up_mat)
        hidden_full_width = lax.optimization_barrier(hidden).astype(jnp.float32)
        lowrank_hidden = jnp.dot(hidden_full_width, first_factor, precision=lax.Precision.HIGHEST)
        base = jnp.dot(hidden, down_mat, preferred_element_type=jnp.float32)
        pruned_row = (base + jnp.dot(lowrank_hidden, second_factor, precision=lax.Precision.HIGHEST)).astype(jnp.bfloat16)
        total = total.at[tok_index].add(pruned_row.astype(jnp.float32) * tok_share[:, None])
        return total, (hidden, lowrank_hidden)

    pruned_estimate, stored_residuals = lax.scan(pruned_update, offset_index, (pruned_token_rows, pruned_gate_weights, gate_weight[0::2], up_weight[0::2], down_weight[0::2], adapter_first_weight, adapter_second_weight))
    residual = pruned_estimate - target

    def gradient_update(carry, inputs):
        tok_index, tok_share, hidden, lowrank_hidden, second_factor = inputs
        grad_row = (jnp.take(residual, tok_index, axis=0) * tok_share[:, None]).astype(jnp.bfloat16)
        gradient_hidden_full = lax.optimization_barrier(grad_row).astype(jnp.float32)
        part_b = jnp.dot(lowrank_hidden.T, gradient_hidden_full, precision=lax.Precision.HIGHEST)
        backward_lowrank = jnp.dot(gradient_hidden_full, second_factor.T, precision=lax.Precision.HIGHEST)
        hidden_full_width = lax.optimization_barrier(hidden).astype(jnp.float32)
        part_a = jnp.dot(hidden_full_width.T, backward_lowrank, precision=lax.Precision.HIGHEST)
        return carry, (part_a, part_b)

    discarded_value, adapter_gradients = lax.scan(gradient_update, jnp.zeros((), jnp.float32), (pruned_token_rows, pruned_gate_weights, stored_residuals[0], stored_residuals[1], adapter_second_weight))
    return adapter_gradients[0], adapter_gradients[1]
```

```python
import functools

import jax
import jax.numpy as jnp
from jax import lax
from jax.experimental import pallas as pl
from jax.experimental.pallas import tpu as pltpu
from jax.sharding import PartitionSpec as P

BF = jnp.bfloat16
F32 = jnp.float32
LANES = 128
NN = (((1,), (0,)), ((), ()))
NT = (((1,), (1,)), ((), ()))
PARAMS = pltpu.CompilerParams(vmem_limit_bytes=48 * 1024 * 1024)


def mm(a, b, dims=NN):
    return lax.dot_general(a, b, dims, preferred_element_type=F32)


def mm_full(a, b, dims=NN):
    return lax.dot_general(a, b, dims, precision=lax.Precision.HIGHEST, preferred_element_type=F32)


def split(v):
    hi = v.astype(BF)
    return hi, (v - hi.astype(F32)).astype(BF)


def cost(flops, nbytes):
    return pl.CostEstimate(flops=flops, bytes_accessed=nbytes, transcendentals=0)


def full_spec(a):
    zeros = (0,) * a.ndim
    return pl.BlockSpec(a.shape, lambda i: zeros)


def hidden_kernel(parts, with_low, x_ref, *refs):
    gates, ups = refs[:parts], refs[parts : 2 * parts]
    depth = gates[0].shape[-2]
    gate = up = None
    for k in range(parts):
        x = x_ref[:, k * depth : (k + 1) * depth]
        g = mm(x, gates[k][...].reshape(gates[k].shape[-2:]))
        u = mm(x, ups[k][...].reshape(ups[k].shape[-2:]))
        gate = g if gate is None else gate + g
        up = u if up is None else up + u
    hidden = (gate / (1.0 + jnp.exp(-gate)) * up).astype(BF)
    if with_low:
        first_ref, coef_ref, h_ref, lt_ref = refs[2 * parts :]
        rank = lt_ref.shape[0]
        both = mm(first_ref[...], hidden, NT)
        lt_ref[...] = (both[:rank] + both[rank:]) * coef_ref[2:3, :]
    else:
        (h_ref,) = refs[2 * parts :]
    h_ref[...] = hidden


def hidden_rows(x, gates, ups, expert, first_t=None, coef=None):
    rows, wide = x.shape
    depth, hid = gates[1].shape
    block = min(256, rows)

    def weight_spec(k):
        if k == 0:
            return pl.BlockSpec((1, depth, hid), lambda i: (expert, 0, 0))
        return pl.BlockSpec((depth, hid), lambda i: (0, 0))

    specs = [pl.BlockSpec((block, wide), lambda i: (i, 0))]
    specs += [weight_spec(k) for k in range(len(gates))] * 2
    args = [x, *gates, *ups]
    out_shape = [jax.ShapeDtypeStruct((rows, hid), BF)]
    out_specs = [pl.BlockSpec((block, hid), lambda i: (i, 0))]
    if first_t is not None:
        args += [first_t, coef]
        specs += [full_spec(first_t), pl.BlockSpec((coef.shape[0], block), lambda i: (0, i))]
        rank = first_t.shape[0] // 2
        out_shape.append(jax.ShapeDtypeStruct((rank, rows), F32))
        out_specs.append(pl.BlockSpec((rank, block), lambda i: (0, i)))
    return pl.pallas_call(
        functools.partial(hidden_kernel, len(gates), first_t is not None),
        grid=(rows // block,),
        in_specs=specs,
        out_specs=out_specs,
        out_shape=out_shape,
        compiler_params=PARAMS,
        cost_estimate=cost(4 * rows * depth * len(gates) * hid, 2 * rows * (wide + hid) + 4 * depth * len(gates) * hid),
        name="hidden_rows",
    )(*args)


def moment_kernel(which, lt_ref, coef_ref, h_ref, hi_ref, lo_ref):
    a_hi, a_lo = split(lt_ref[...] * coef_ref[which : which + 1, :])
    h = h_ref[...]
    hi, lo = split(mm(a_hi, h) + mm(a_lo, h))
    hi_ref[...] = hi
    lo_ref[...] = lo


def moments(lt_all, coef, h, which):
    total, rows = lt_all.shape
    hid = h.shape[1]
    block = 256
    return pl.pallas_call(
        functools.partial(moment_kernel, which),
        grid=(total // block,),
        in_specs=[pl.BlockSpec((block, rows), lambda i: (i, 0)), full_spec(coef), full_spec(h)],
        out_specs=[pl.BlockSpec((block, hid), lambda i: (i, 0))] * 2,
        out_shape=[jax.ShapeDtypeStruct((total, hid), BF)] * 2,
        compiler_params=PARAMS,
        cost_estimate=cost(4 * total * rows * hid, 4 * total * (rows + hid) + 2 * rows * hid),
        name="moments",
    )(lt_all, coef, h)


def slice_kernel(
    carry, hi0_ref, lo0_ref, hi1_ref, lo1_ref, d0_ref, d1_ref, n_ref, own_ref, all_ref, *refs
):
    d0 = d0_ref[...].reshape(d0_ref.shape[-2:])
    d1 = d1_ref[...].reshape(d1_ref.shape[-2:])
    g_ref, k0_ref, k1_ref = refs[-3:]
    g = mm(hi0_ref[...], d0) + mm(lo0_ref[...], d0) + mm(hi1_ref[...], d1) + mm(lo1_ref[...], d1)
    n_hi, n_lo = split(n_ref[...])
    o_hi, o_lo = split(own_ref[...])
    g_ref[...] = g + mm(n_hi, o_hi) + mm(n_lo, o_hi) + mm(n_hi, o_lo)
    a_hi, a_lo = split(all_ref[...])
    k0 = mm(a_hi, d0, NT) + mm(a_lo, d0, NT)
    k1 = mm(a_hi, d1, NT) + mm(a_lo, d1, NT)
    if carry:
        k0 = k0 + refs[0][...]
        k1 = k1 + refs[1][...]
    k0_ref[...] = k0
    k1_ref[...] = k1


def slice_step(m0, m1, d0, d1, n, second, second_all, k, keys):
    total, hid = m0[0].shape
    depth = d0.shape[-1]
    rank = second.shape[0]
    block = 256
    row = lambda width: pl.BlockSpec((block, width), lambda i: (i, 0))

    def down_spec(d, expert):
        if d.ndim == 3:
            return pl.BlockSpec((1, hid, depth), lambda i: (expert, 0, 0))
        return full_spec(d)

    specs = [row(hid)] * 4 + [down_spec(d0, 0), down_spec(d1, 1), row(rank)]
    specs += [pl.BlockSpec((rank, depth), lambda i: (0, k)), pl.BlockSpec((block, depth), lambda i: (i, k))]
    args = [*m0, *m1, d0, d1, n, second, second_all]
    if keys is not None:
        args += list(keys)
        specs += [row(hid)] * 2
    g, k0, k1 = pl.pallas_call(
        functools.partial(slice_kernel, keys is not None),
        grid=(total // block,),
        in_specs=specs,
        out_specs=[row(depth), row(hid), row(hid)],
        out_shape=[
            jax.ShapeDtypeStruct((total, depth), F32),
            jax.ShapeDtypeStruct((total, hid), F32),
            jax.ShapeDtypeStruct((total, hid), F32),
        ],
        compiler_params=PARAMS,
        cost_estimate=cost(16 * total * hid * depth, 16 * total * hid + 8 * total * depth + 4 * hid * depth),
        name="down_slice",
    )(*args)
    return g, (k0, k1)


def back_kernel(k0_ref, k1_ref, h0_ref, h1_ref, coef_ref, s_ref, lt_ref, b_ref):
    k_hi, k_lo = split(k0_ref[...])
    h = h0_ref[...]
    b = (mm(k_hi, h, NT) + mm(k_lo, h, NT)) * coef_ref[0:1, :]
    k_hi, k_lo = split(k1_ref[...])
    h = h1_ref[...]
    b += (mm(k_hi, h, NT) + mm(k_lo, h, NT)) * coef_ref[1:2, :]
    s_hi, s_lo = split(s_ref[...])
    l_hi, l_lo = split(lt_ref[...])
    b_ref[...] = b + mm(s_hi, l_hi) + mm(s_lo, l_hi) + mm(s_hi, l_lo)


def back_rows(keys, h0, h1, coef, s, lt):
    total, hid = keys[0].shape
    rows = h0.shape[0]
    rank = s.shape[1]
    block = 256
    row = lambda width: pl.BlockSpec((block, width), lambda i: (i, 0))
    return pl.pallas_call(
        back_kernel,
        grid=(total // block,),
        in_specs=[row(hid), row(hid), full_spec(h0), full_spec(h1), full_spec(coef), row(rank), full_spec(lt)],
        out_specs=row(rows),
        out_shape=jax.ShapeDtypeStruct((total, rows), F32),
        compiler_params=PARAMS,
        cost_estimate=cost(8 * total * rows * hid, 8 * total * hid + 4 * rows * hid + 4 * total * rows),
        name="back_rows",
    )(keys[0], keys[1], h0, h1, coef, s, lt)


def swap(v, axis, mask):
    size = lax.axis_size(axis)
    return lax.ppermute(v, axis, [(i, i ^ mask) for i in range(size)])


def spread(own, low_first):
    size = lax.axis_size("dp")
    got = [own]
    for k in range(1, size):
        bit = 1 << (k.bit_length() - 1) if low_first else k & -k
        got.append(swap(got[k ^ bit], "dp", bit))
    return got


def sum_over_experts(v):
    size = lax.axis_size("expert")
    v = v.reshape(size // 2, 2, *v.shape[1:])
    chip = v[:, 0] + swap(v[:, 1], "expert", 1)
    total = chip[0]
    for m in range(1, size // 2):
        total = total + swap(chip[m], "expert", 2 * m)
    return total


def relative(v, axis_name):
    me = lax.axis_index(axis_name)
    return jnp.concatenate(
        [lax.dynamic_slice_in_dim(v, me ^ r, 1, 0) for r in range(v.shape[0])], axis=0
    )


def shares_of(index, scores, count):
    shares = scores / jnp.sum(scores, axis=1, keepdims=True)
    hit = index[:, :, None] == jnp.arange(count, dtype=jnp.int32)[None, None, :]
    return jnp.sum(jnp.where(hit, shares[:, :, None], 0.0), axis=1)


def shards(
    tokens,
    initial_expert_index,
    pruned_expert_index,
    initial_router_scores,
    pruned_router_scores,
    gate_weight,
    up_weight,
    down_weight,
    adapter_first_weight,
    adapter_second_weight,
):
    peers = lax.axis_size("expert")
    groups = lax.axis_size("dp")
    place = lax.axis_index("dp")
    me = lax.axis_index("expert")
    tok, width = tokens.shape
    hid = gate_weight.shape[2]
    depth = gate_weight.shape[1]
    rank = adapter_first_weight.shape[2]

    gates, ups = [], []
    for e in range(2):
        gates.append(spread(gate_weight[e], True))
        ups.append(spread(up_weight[e], False))

    frozen = shares_of(initial_expert_index, initial_router_scores, 2 * peers).reshape(tok, peers, 2)
    kept = shares_of(pruned_expert_index, pruned_router_scores, peers)
    table = jnp.stack([kept - frozen[:, :, 0], -frozen[:, :, 1], kept], axis=2).reshape(tok, 3 * peers)
    t_hi, rest = table.astype(BF), table
    rest = rest - t_hi.astype(F32)
    t_mid = rest.astype(BF)
    t_lo = (rest - t_mid.astype(F32)).astype(BF)
    table = jnp.concatenate([t_hi, t_mid, t_lo], axis=1)
    pad = -table.shape[1] % LANES
    table = jnp.pad(table, ((0, 0), (0, pad)))

    def turned(v):
        return jnp.concatenate(
            [lax.dynamic_slice_in_dim(v, (place ^ k) * depth, depth, 1) for k in range(groups)], axis=1
        )

    packet = jnp.concatenate([turned(tokens), table], axis=1)
    x = lax.all_gather(packet, "expert", axis=0, tiled=True)
    second = turned(adapter_second_weight[0])
    second_all = lax.all_gather(second, "expert", axis=0)
    second_all = relative(second_all, "expert").reshape(peers * rank, width)

    column = jnp.arange(table.shape[1], dtype=jnp.int32)[None, :]
    kind = jnp.arange(8, dtype=jnp.int32)[:, None]
    pick = (column % (3 * peers) == 3 * me + kind) & (kind < 3) & (column < 9 * peers)
    coef = mm(pick.astype(BF), x[:, width:], NT)

    first_t = jnp.concatenate(split(adapter_first_weight[0].T), axis=0)
    own_gate, own_up = gate_weight, up_weight
    h0, lt = hidden_rows(x, [own_gate, *gates[0][1:]], [own_up, *ups[0][1:]], 0, first_t, coef)
    lt_all = lax.all_gather(lt, "expert", axis=0)
    lt_all = relative(lt_all, "expert").reshape(peers * rank, peers * tok)
    (h1,) = hidden_rows(x, [own_gate, *gates[1][1:]], [own_up, *ups[1][1:]], 1)
    m0 = moments(lt_all, coef, h0, 0)
    m1 = moments(lt_all, coef, h1, 1)
    n = mm_full(lt_all, lt, NT)
    s = mm_full(second_all, second, NT)

    downs = [spread(down_weight[0], True), spread(down_weight[1], False)]
    keys, parts = None, []
    for k in range(groups):
        d0, d1 = (down_weight, down_weight) if k == 0 else (downs[0][k], downs[1][k])
        g, keys = slice_step(m0, m1, d0, d1, n, second, second_all, k, keys)
        g = sum_over_experts(g.reshape(peers, rank, depth))
        parts.append(g if k == 0 else swap(g, "dp", k))
    grad_b = functools.reduce(jnp.add, parts)

    b = back_rows(keys, h0, h1, coef, s, lt)
    b = sum_over_experts(b.reshape(peers, rank, peers * tok)) * coef[2:3, :]
    over_tokens = (((0,), (1,)), ((), ()))
    b_hi, b_lo = split(b)
    part_a = mm(h0, b_hi, over_tokens) + mm(h0, b_lo, over_tokens)
    rows = hid // groups
    grad_a = lax.dynamic_slice_in_dim(part_a, place * rows, rows, 0)
    for k in range(1, groups):
        grad_a = grad_a + swap(lax.dynamic_slice_in_dim(part_a, (place ^ k) * rows, rows, 0), "dp", k)
    return grad_a[None], grad_b[None]


def solution(mesh):
    placed = (
        P(("dp", "expert"), None),
        P(("dp", "expert"), None),
        P(("dp", "expert"), None),
        P(("dp", "expert"), None),
        P(("dp", "expert"), None),
        P("expert", "dp", None),
        P("expert", "dp", None),
        P("expert", None, "dp"),
        P("expert", None, None),
        P("expert", None, None),
    )
    return jax.shard_map(
        shards,
        mesh=mesh,
        in_specs=placed,
        out_specs=(P("expert", "dp", None), P("expert", None, "dp")),
        check_vma=False,
    )
```

```python
import functools

import jax
import jax.numpy as jnp
from jax import lax
from jax.experimental import pallas as pl
from jax.experimental.pallas import tpu as pltpu
from jax.sharding import PartitionSpec as P

BF = jnp.bfloat16
F32 = jnp.float32
LANES = 128
NN = (((1,), (0,)), ((), ()))
NT = (((1,), (1,)), ((), ()))
PARAMS = pltpu.CompilerParams(vmem_limit_bytes=48 * 1024 * 1024)


def mm(a, b, dims=NN):
    return lax.dot_general(a, b, dims, preferred_element_type=F32)


def mm_full(a, b, dims=NN):
    return lax.dot_general(a, b, dims, precision=lax.Precision.HIGHEST, preferred_element_type=F32)


def split(v):
    hi = v.astype(BF)
    return hi, (v - hi.astype(F32)).astype(BF)


def stacked(v):
    return jnp.concatenate(split(v), axis=0)


def mm_split(a, b, dims=NN):
    both = mm(a, b, dims)
    half = a.shape[0] // 2
    return both[:half] + both[half:]


def cost(flops, nbytes):
    return pl.CostEstimate(flops=flops // 1000, bytes_accessed=nbytes // 1000, transcendentals=0)


def full_spec(a):
    zeros = (0,) * a.ndim
    return pl.BlockSpec(a.shape, lambda i, *at: zeros)


def columns(at_ref, k, depth):
    return pl.ds(pl.multiple_of((at_ref[2] ^ k) * depth, LANES), depth)


def as_matrix(ref):
    return ref[...].reshape(ref.shape[-2:])


def halving(chips):
    order = [0]
    while len(order) < chips:
        order = [2 * m for m in order] + [2 * m + 1 for m in order]
    return order


def relative_specs(blocks, start):
    def spec(m):
        return pl.BlockSpec((1, *blocks.shape[1:]), lambda i, at: (at[3] ^ (2 * m + i + start), 0, 0))

    return [spec(m) for m in halving(blocks.shape[0] // 2)]


def rows_of(refs):
    return jnp.concatenate([ref[0] for ref in refs], axis=0)


def placed_spec(item):
    arr, index = item
    return pl.BlockSpec((1, *arr.shape[1:]), lambda *_: (index, 0, 0))


def hidden_kernel(ks, carry, finish, low, at_ref, x_ref, *refs):
    refs = list(refs)
    gates = [refs.pop(0) for _ in ks]
    ups = [refs.pop(0) for _ in ks]
    gate, up = (refs.pop(0)[...], refs.pop(0)[...]) if carry else (None, None)
    depth = gates[0].shape[1]
    for k, g_ref, u_ref in zip(ks, gates, ups):
        x = x_ref[:, columns(at_ref, k, depth)] if x_ref.shape[1] > depth else x_ref[...]
        g = mm(x, as_matrix(g_ref))
        u = mm(x, as_matrix(u_ref))
        gate = g if gate is None else gate + g
        up = u if up is None else up + u
    if not finish:
        gate_ref, up_ref = refs
        gate_ref[...] = gate
        up_ref[...] = up
        return
    hidden = (gate / (1.0 + jnp.exp(-gate)) * up).astype(BF)
    if low:
        first_ref, pick_ref, h_ref, lt_ref, coef_ref = refs
        rank = lt_ref.shape[0]
        coef = mm(pick_ref[...], x_ref[:, x_ref.shape[1] - pick_ref.shape[1] :], NT)
        both = mm(first_ref[...], hidden, NT)
        lt_ref[...] = (both[:rank] + both[rank:]) * coef[2:3, :]
        coef_ref[...] = coef
    else:
        (h_ref,) = refs
    h_ref[...] = hidden


def hidden_rows(at, x, items, ks, sums=(), finish=True, first_t=None, pick=None):
    rows, wide = x.shape
    depth, hid = items[0][0][0].shape[1:]
    block = min(256, rows)
    items = [items[k][p] for p in range(2) for k in ks]
    if len(ks) == 1:
        specs = [pl.BlockSpec((block, depth), lambda i, at: (i, at[2] ^ ks[0]))]
        wide = depth
    else:
        specs = [pl.BlockSpec((block, wide), lambda i, at: (i, 0))]
    specs += [placed_spec(item) for item in items]
    row = pl.BlockSpec((block, hid), lambda i, at: (i, 0))
    specs += [row] * len(sums)
    args = [x, *(arr for arr, _ in items), *sums]
    if not finish:
        out_shape = [jax.ShapeDtypeStruct((rows, hid), F32)] * 2
        out_specs = [row, row]
    else:
        out_shape = [jax.ShapeDtypeStruct((rows, hid), BF)]
        out_specs = [row]
    if first_t is not None:
        args += [first_t, pick]
        specs += [full_spec(first_t), full_spec(pick)]
        for count in (first_t.shape[0] // 2, pick.shape[0]):
            out_shape.append(jax.ShapeDtypeStruct((count, rows), F32))
            out_specs.append(pl.BlockSpec((count, block), lambda i, at: (0, i)))
    return pl.pallas_call(
        functools.partial(hidden_kernel, ks, len(sums) > 0, finish, first_t is not None),
        grid_spec=pltpu.PrefetchScalarGridSpec(
            num_scalar_prefetch=1,
            grid=(rows // block,),
            in_specs=specs,
            out_specs=out_specs,
        ),
        out_shape=out_shape,
        compiler_params=PARAMS,
        cost_estimate=cost(4 * rows * depth * len(ks) * hid, rows * (2 * wide + 2 * hid) + 4 * depth * len(ks) * hid),
        name="hidden_rows",
    )(at, *args)


def moment_kernel(at_ref, *refs):
    coef_ref, h0_ref, h1_ref, own_ref, m0_ref, m1_ref, n_ref = refs[-7:]
    lt = rows_of(refs[:-7])
    for which, h_ref, m_ref in ((0, h0_ref, m0_ref), (1, h1_ref, m1_ref)):
        hi, lo = split(mm_split(stacked(lt * coef_ref[which : which + 1, :]), h_ref[...]))
        m_ref[0] = hi
        m_ref[1] = lo
    a_hi, a_lo = split(lt)
    b_hi, b_lo = split(own_ref[...])
    n_ref[...] = mm(a_hi, b_hi, NT) + mm(a_lo, b_hi, NT) + mm(a_hi, b_lo, NT)


def moments(at, lows, coef, h0, h1, lt):
    peers, rank, rows = lows.shape
    hid = h0.shape[1]
    total, block = peers * rank, peers * rank // 2
    terms = pl.BlockSpec((2, block, hid), lambda i, at: (0, i, 0))
    specs = relative_specs(lows, 0)
    return pl.pallas_call(
        moment_kernel,
        grid_spec=pltpu.PrefetchScalarGridSpec(
            num_scalar_prefetch=1,
            grid=(2,),
            in_specs=[*specs, full_spec(coef), full_spec(h0), full_spec(h1), full_spec(lt)],
            out_specs=[terms, terms, pl.BlockSpec((block, rank), lambda i, at: (i, 0))],
        ),
        out_shape=[jax.ShapeDtypeStruct((2, total, hid), BF)] * 2 + [jax.ShapeDtypeStruct((total, rank), F32)],
        compiler_params=PARAMS,
        cost_estimate=cost(8 * total * rows * hid, 4 * total * (rows + 2 * hid) + 4 * rows * hid),
        name="moments",
    )(at, *[lows] * len(specs), coef, h0, h1, lt)


def grad_kernel(ks, at_ref, m0_ref, m1_ref, n_ref, second_ref, *refs):
    m0, m1 = (m_ref[...].reshape(-1, m_ref.shape[2]) for m_ref in (m0_ref, m1_ref))
    n_hi, n_lo = split(n_ref[...])
    outs = refs[2 * len(ks) :]
    for p, k in enumerate(ks):
        d0, d1 = as_matrix(refs[2 * p]), as_matrix(refs[2 * p + 1])
        o_hi, o_lo = split(second_ref[:, columns(at_ref, k, d0.shape[1])])
        g = mm_split(m0, d0) + mm_split(m1, d1)
        outs[0][:, p * d0.shape[1] : (p + 1) * d0.shape[1]] = g + mm(n_hi, o_hi) + mm(n_lo, o_hi) + mm(n_hi, o_lo)


def grad_sums(at, ms, n, downs, second, ks, start, total):
    hid = ms[0].shape[2]
    rank = second.shape[0]
    depth = downs[0][0][0].shape[2]
    block = min(256, total)
    row = lambda width: pl.BlockSpec((block, width), lambda i, *at: (i + start // block, 0))
    terms = pl.BlockSpec((2, block, hid), lambda i, *at: (0, i + start // block, 0))
    args, specs = [*ms, n, second], [terms, terms, row(rank), full_spec(second)]
    for k in ks:
        args += [arr for arr, _ in downs[k]]
        specs += [placed_spec(item) for item in downs[k]]
    return pl.pallas_call(
        functools.partial(grad_kernel, ks),
        grid_spec=pltpu.PrefetchScalarGridSpec(
            num_scalar_prefetch=1,
            grid=(total // block,),
            in_specs=specs,
            out_specs=pl.BlockSpec((block, len(ks) * depth), lambda i, *at: (i, 0)),
        ),
        out_shape=jax.ShapeDtypeStruct((total, len(ks) * depth), F32),
        compiler_params=PARAMS,
        cost_estimate=cost(8 * total * hid * depth * len(ks), 8 * total * hid + 4 * len(ks) * depth * (total + hid)),
        name="grad_sums",
    )(at, *args)


def key_terms(at_ref, sec_refs, d, k):
    where = columns(at_ref, k, d.shape[1])
    sec = jnp.concatenate([ref[0, :, where] for ref in sec_refs], axis=0)
    return mm_split(stacked(sec), d, NT)


def key_kernel(ks, at_ref, *refs):
    *refs, own_ref, k0_ref, k1_ref, s_ref = refs
    sec_refs, downs = refs[: -2 * len(ks)], refs[-2 * len(ks) :]
    for e, out_ref in enumerate((k0_ref, k1_ref)):
        key = None
        for p, k in enumerate(ks):
            term = key_terms(at_ref, sec_refs, as_matrix(downs[2 * p + e]), k)
            key = term if key is None else key + term
        out_ref[...] = key
    hi, lo = split(rows_of(sec_refs))
    own_hi, own_lo = split(own_ref[...])
    s_ref[...] = mm(hi, own_hi, NT) + mm(lo, own_hi, NT) + mm(hi, own_lo, NT)


def key_sums(at, seconds, second, downs, ks):
    peers, rank, width = seconds.shape
    depth = downs[0][0][0].shape[2]
    hid = downs[0][0][0].shape[1]
    total, block = peers * rank, peers * rank // 2
    row = lambda wide: pl.BlockSpec((block, wide), lambda i, at: (i, 0))
    specs = relative_specs(seconds, 0)
    args = [seconds] * len(specs)
    for k in ks:
        args += [arr for arr, _ in downs[k]]
        specs += [placed_spec(item) for item in downs[k]]
    return pl.pallas_call(
        functools.partial(key_kernel, ks),
        grid_spec=pltpu.PrefetchScalarGridSpec(
            num_scalar_prefetch=1,
            grid=(2,),
            in_specs=[*specs, full_spec(second)],
            out_specs=[row(hid), row(hid), row(rank)],
        ),
        out_shape=[jax.ShapeDtypeStruct((total, hid), F32)] * 2 + [jax.ShapeDtypeStruct((total, rank), F32)],
        compiler_params=PARAMS,
        cost_estimate=cost(8 * total * hid * len(ks) * depth, 4 * total * (width + 2 * hid)),
        name="key_sums",
    )(at, *args, second)


def back_kernel(last, at_ref, *refs):
    *sec_refs, d0_ref, d1_ref, k0_ref, k1_ref, h0_ref, h1_ref, coef_ref, s_ref, lt_ref, b_ref = refs
    b = None
    for e, d_ref, k_ref, h_ref in ((0, d0_ref, k0_ref, h0_ref), (1, d1_ref, k1_ref, h1_ref)):
        key = k_ref[...] + key_terms(at_ref, sec_refs, as_matrix(d_ref), last)
        term = mm_split(stacked(key), h_ref[...], NT) * coef_ref[e : e + 1, :]
        b = term if b is None else b + term
    s_hi, s_lo = split(s_ref[...])
    l_hi, l_lo = split(lt_ref[...])
    b_ref[...] = b + mm(s_hi, l_hi) + mm(s_lo, l_hi) + mm(s_hi, l_lo)


def back_rows(at, seconds, down, last, keys, s, h0, h1, coef, lt, side):
    hid = keys[0].shape[1]
    rows = h0.shape[0]
    rank = s.shape[1]
    block = s.shape[0] // 2
    row = lambda width: pl.BlockSpec((block, width), lambda i, at: (side, 0))
    specs = relative_specs(seconds, side)
    args = [seconds] * len(specs)
    specs += [*(placed_spec(item) for item in down), row(hid), row(hid)]
    specs += [full_spec(h0), full_spec(h1), full_spec(coef), row(rank), full_spec(lt)]
    return pl.pallas_call(
        functools.partial(back_kernel, last),
        grid_spec=pltpu.PrefetchScalarGridSpec(
            num_scalar_prefetch=1,
            grid=(1,),
            in_specs=specs,
            out_specs=pl.BlockSpec((block, rows), lambda i, at: (0, 0)),
        ),
        out_shape=jax.ShapeDtypeStruct((block, rows), F32),
        compiler_params=PARAMS,
        cost_estimate=cost(8 * block * rows * hid, 8 * block * hid + 4 * rows * hid + 4 * block * rows),
        name="back_rows",
    )(at, *args, *(arr for arr, _ in down), *keys, h0, h1, coef, s, lt)


def swap(v, axis, mask):
    size = lax.axis_size(axis)
    return lax.ppermute(v, axis, [(i, i ^ mask) for i in range(size)])


def after(v, *done):
    return lax.optimization_barrier((v, *done))[0] if done else v


def spread(own, orders, wait=(), passing=()):
    size = lax.axis_size("dp")
    got = [[(own, p) for p in range(len(orders))]]
    for k in range(1, size):
        if k & (k - 1) == 0:
            sent = swap(after(own, *wait), "dp", k)
            got.append([(sent, p) for p in range(len(orders))])
            continue
        items = []
        for p, highest_last in enumerate(orders):
            bit = 1 << (k.bit_length() - 1) if highest_last else k & -k
            arr, place = got[k ^ bit][p]
            items.append((swap(after(arr[place : place + 1], *passing), "dp", bit), 0))
        got.append(items)
    return got


def chip_blocks(v, waits):
    got = [v]
    for m in range(1, lax.axis_size("expert") // 2):
        bit = m & -m if m & 1 else m
        got.append(swap(after(got[m ^ bit], *waits.get(m, ())), "expert", 2 * bit))
    return got


def both_cores(blocks):
    mine = jnp.stack(blocks)
    return mine, swap(mine, "expert", 1)


def sum_over_experts(near, far, dtype=F32):
    return sum_over_chips(near + swap(far, "expert", 1), dtype)


def sum_over_chips(total, dtype):
    mask = 2
    while total.shape[0] > 1:
        half = total.shape[0] // 2
        total = total[:half] + swap(total[half:].astype(dtype), "expert", mask).astype(F32)
        mask *= 2
    return total[0]


def shares_of(index, scores, count):
    shares = scores / jnp.sum(scores, axis=1, keepdims=True)
    hit = index[:, :, None] == jnp.arange(count, dtype=jnp.int32)[None, None, :]
    return jnp.sum(jnp.where(hit, shares[:, :, None], 0.0), axis=1)


def shards(
    tokens,
    initial_expert_index,
    pruned_expert_index,
    initial_router_scores,
    pruned_router_scores,
    gate_weight,
    up_weight,
    down_weight,
    adapter_first_weight,
    adapter_second_weight,
):
    peers = lax.axis_size("expert")
    groups = lax.axis_size("dp")
    place = lax.axis_index("dp")
    me = lax.axis_index("expert")
    chips = peers // 2
    tok, width = tokens.shape
    hid = gate_weight.shape[2]
    depth = gate_weight.shape[1]
    rank = adapter_first_weight.shape[2]

    frozen = shares_of(initial_expert_index, initial_router_scores, 2 * peers).reshape(tok, peers, 2)
    kept = shares_of(pruned_expert_index, pruned_router_scores, peers)
    table = jnp.stack([kept - frozen[:, :, 0], -frozen[:, :, 1], kept], axis=2).reshape(tok, 3 * peers)
    t_hi, rest = table.astype(BF), table
    rest = rest - t_hi.astype(F32)
    t_mid = rest.astype(BF)
    t_lo = (rest - t_mid.astype(F32)).astype(BF)
    table = jnp.concatenate([t_hi, t_mid, t_lo], axis=1)
    table = jnp.pad(table, ((0, 0), (0, -table.shape[1] % LANES)))

    column = jnp.arange(table.shape[1], dtype=jnp.int32)[None, :]
    kind = jnp.arange(8, dtype=jnp.int32)[:, None]
    pick = ((column % (3 * peers) == 3 * me + kind) & (kind < 3) & (column < 9 * peers)).astype(BF)
    at = jnp.stack([me // 2, me % 2, place, me]).astype(jnp.int32)
    first_t = jnp.concatenate(split(adapter_first_weight[0].T), axis=0)
    second = adapter_second_weight[0]

    last = groups - 1
    most = list(range(last))
    def direct(got):
        return [got[1 << p][0][0] for p in range(groups.bit_length() - 1)]

    def ends(got):
        return [arr for arr, _ in got[last]]

    def both(first, second):
        return [a + b for a, b in zip(first, second)]

    def with_own(got, *own):
        return [list(own)] + got[1:]

    pair0 = spread(jnp.stack([gate_weight[0], up_weight[0]]), (True, False))
    w0 = with_own(pair0, (gate_weight, 0), (up_weight, 0))

    packet = jnp.concatenate([tokens, table], axis=1)
    x = lax.all_gather(packet, "expert", axis=0, tiled=True)
    seconds = lax.all_gather(after(second, *direct(pair0)), "expert", axis=0)
    h0, lt, coef = hidden_rows(at, x, w0, most + [last], (), True, first_t, pick)

    pair1 = spread(jnp.stack([gate_weight[1], up_weight[1]]), (True, False), ends(pair0))
    w1 = with_own(pair1, (gate_weight, 1), (up_weight, 1))
    lows = lax.all_gather(after(lt, *direct(pair1), seconds), "expert", axis=0)
    sums = hidden_rows(at, x, w1, most, (), False)
    (h1,) = hidden_rows(at, x, w1, [last], sums)
    *ms, n = moments(at, lows, coef, h0, h1, lt)

    down0 = spread(down_weight[0:1], (True,), direct(pair1), (n,))
    down1 = spread(down_weight[1:2], (False,), (sums[0],), (n,))
    downs = with_own(both(down0, down1), (down_weight, 0), (down_weight, 1))

    half = chips * rank

    def grad_part(ms, ks):
        far, near = (
            grad_sums(at, ms, n, downs, second, ks, start, half).reshape(chips, rank, len(ks) * depth)
            for start in (half, 0)
        )
        return far, near

    far, near = grad_part(ms, [0])
    swapped = [near + swap(far, "expert", 1)]
    *keys, s = key_sums(at, seconds, after(second, near), downs, most)
    far, near = grad_part([after(ms[0], s), ms[1]], most[1:])
    swapped.append(near + swap(far, "expert", 1))
    seconds_late = after(seconds, near)

    far, near = (
        back_rows(at, seconds_late, downs[last], last, keys, s, h0, h1, coef, lt, side) for side in (1, 0)
    )
    b = near.reshape(chips, rank, peers * tok) + swap(far.reshape(chips, rank, peers * tok), "expert", 1)
    early = sum_over_chips(after(jnp.concatenate(swapped, axis=2), b), BF)
    far, near = grad_part([after(ms[0], b), *ms[1:]], [last])
    b = sum_over_chips(b, F32) * coef[2:3, :]
    late = sum_over_experts(near, far, BF)

    over_tokens = (((0,), (1,)), ((), ()))
    b_hi, b_lo = split(b)
    part_a = mm(h0, b_hi, over_tokens) + mm(h0, b_lo, over_tokens)
    rows = hid // groups
    grad_a = lax.dynamic_slice_in_dim(part_a, place * rows, rows, 0)
    for k in range(1, groups):
        grad_a = grad_a + swap(lax.dynamic_slice_in_dim(part_a, (place ^ k) * rows, rows, 0), "dp", k)
    grad_b = early[:, :depth]
    for k in range(1, groups):
        part = late if k == last else early[:, k * depth : (k + 1) * depth]
        grad_b = grad_b + swap(part, "dp", k)
    return grad_a[None], grad_b[None]


def solution(mesh):
    placed = (
        P(("dp", "expert"), None),
        P(("dp", "expert"), None),
        P(("dp", "expert"), None),
        P(("dp", "expert"), None),
        P(("dp", "expert"), None),
        P("expert", "dp", None),
        P("expert", "dp", None),
        P("expert", None, "dp"),
        P("expert", None, None),
        P("expert", None, None),
    )
    return jax.shard_map(
        shards,
        mesh=mesh,
        in_specs=placed,
        out_specs=(P("expert", "dp", None), P("expert", None, "dp")),
        check_vma=False,
    )
```

```python
import functools

import jax
import jax.numpy as jnp
from jax import lax
from jax.experimental import pallas as pl
from jax.experimental.pallas import tpu as pltpu
from jax.sharding import PartitionSpec as P

BF = jnp.bfloat16
F32 = jnp.float32
LANES = 128
NN = (((1,), (0,)), ((), ()))
NT = (((1,), (1,)), ((), ()))
PARAMS = pltpu.CompilerParams(vmem_limit_bytes=48 * 1024 * 1024)


def mm(a, b, dims=NN):
    return lax.dot_general(a, b, dims, preferred_element_type=F32)


def mm_full(a, b, dims=NN):
    return lax.dot_general(a, b, dims, precision=lax.Precision.HIGHEST, preferred_element_type=F32)


def split(v):
    hi = v.astype(BF)
    return hi, (v - hi.astype(F32)).astype(BF)


def stacked(v):
    return jnp.concatenate(split(v), axis=0)


def mm_split(a, b, dims=NN):
    both = mm(a, b, dims)
    half = a.shape[0] // 2
    return both[:half] + both[half:]


def cost(flops, nbytes):
    return pl.CostEstimate(flops=flops // 1000, bytes_accessed=nbytes // 1000, transcendentals=0)


def full_spec(a):
    zeros = (0,) * a.ndim
    return pl.BlockSpec(a.shape, lambda i, *at: zeros)


def columns(at_ref, k, depth):
    return pl.ds(pl.multiple_of((at_ref[2] ^ k) * depth, LANES), depth)


def as_matrix(ref):
    return ref[...].reshape(ref.shape[-2:])


def halving(chips):
    order = [0]
    while len(order) < chips:
        order = [2 * m for m in order] + [2 * m + 1 for m in order]
    return order


def relative_specs(blocks, start, k=None, depth=None):
    def spec(m):
        if k is not None:
            return pl.BlockSpec(
                (1, blocks.shape[1], depth), lambda i, at: (at[3] ^ (2 * m + i + start), 0, at[2] ^ k)
            )
        return pl.BlockSpec((1, *blocks.shape[1:]), lambda i, at: (at[3] ^ (2 * m + i + start), 0, 0))

    return [spec(m) for m in halving(blocks.shape[0] // 2)]


def rows_of(refs):
    return jnp.concatenate([ref[0] for ref in refs], axis=0)


def placed_spec(item):
    arr, index = item
    return pl.BlockSpec((1, *arr.shape[1:]), lambda *_: (index, 0, 0))


def hidden_kernel(ks, carry, finish, low, at_ref, x_ref, *refs):
    refs = list(refs)
    gates = [refs.pop(0) for _ in ks]
    ups = [refs.pop(0) for _ in ks]
    gate, up = (refs.pop(0)[...], refs.pop(0)[...]) if carry else (None, None)
    depth = gates[0].shape[1]
    for k, g_ref, u_ref in zip(ks, gates, ups):
        x = x_ref[:, columns(at_ref, k, depth)] if x_ref.shape[1] > depth else x_ref[...]
        g = mm(x, as_matrix(g_ref))
        u = mm(x, as_matrix(u_ref))
        gate = g if gate is None else gate + g
        up = u if up is None else up + u
    if not finish:
        gate_ref, up_ref = refs
        gate_ref[...] = gate
        up_ref[...] = up
        return
    hidden = (gate / (1.0 + jnp.exp(-gate)) * up).astype(BF)
    if low:
        first_ref, pick_ref, h_ref, lt_ref, coef_ref = refs
        rank = lt_ref.shape[0]
        coef = mm(pick_ref[...], x_ref[:, x_ref.shape[1] - pick_ref.shape[1] :], NT)
        both = mm(first_ref[...], hidden, NT)
        lt_ref[...] = (both[:rank] + both[rank:]) * coef[2:3, :]
        coef_ref[...] = coef
    else:
        (h_ref,) = refs
    h_ref[...] = hidden


def hidden_rows(at, x, items, ks, sums=(), finish=True, first_t=None, pick=None):
    rows, wide = x.shape
    depth, hid = items[0][0][0].shape[1:]
    block = min(256, rows)
    items = [items[k][p] for p in range(2) for k in ks]
    if len(ks) == 1:
        specs = [pl.BlockSpec((block, depth), lambda i, at: (i, at[2] ^ ks[0]))]
        wide = depth
    else:
        specs = [pl.BlockSpec((block, wide), lambda i, at: (i, 0))]
    specs += [placed_spec(item) for item in items]
    row = pl.BlockSpec((block, hid), lambda i, at: (i, 0))
    specs += [row] * len(sums)
    args = [x, *(arr for arr, _ in items), *sums]
    if not finish:
        out_shape = [jax.ShapeDtypeStruct((rows, hid), F32)] * 2
        out_specs = [row, row]
    else:
        out_shape = [jax.ShapeDtypeStruct((rows, hid), BF)]
        out_specs = [row]
    if first_t is not None:
        args += [first_t, pick]
        specs += [full_spec(first_t), full_spec(pick)]
        for count in (first_t.shape[0] // 2, pick.shape[0]):
            out_shape.append(jax.ShapeDtypeStruct((count, rows), F32))
            out_specs.append(pl.BlockSpec((count, block), lambda i, at: (0, i)))
    return pl.pallas_call(
        functools.partial(hidden_kernel, ks, len(sums) > 0, finish, first_t is not None),
        grid_spec=pltpu.PrefetchScalarGridSpec(
            num_scalar_prefetch=1,
            grid=(rows // block,),
            in_specs=specs,
            out_specs=out_specs,
        ),
        out_shape=out_shape,
        compiler_params=PARAMS,
        cost_estimate=cost(4 * rows * depth * len(ks) * hid, rows * (2 * wide + 2 * hid) + 4 * depth * len(ks) * hid),
        name="hidden_rows",
    )(at, *args)


def moment_kernel(at_ref, *refs):
    coef_ref, h0_ref, h1_ref, own_ref, m0_ref, m1_ref, n_ref = refs[-7:]
    lt = rows_of(refs[:-7])
    for which, h_ref, m_ref in ((0, h0_ref, m0_ref), (1, h1_ref, m1_ref)):
        hi, lo = split(mm_split(stacked(lt * coef_ref[which : which + 1, :]), h_ref[...]))
        m_ref[0] = hi
        m_ref[1] = lo
    a_hi, a_lo = split(lt)
    b_hi, b_lo = split(own_ref[...])
    n_ref[...] = mm(a_hi, b_hi, NT) + mm(a_lo, b_hi, NT) + mm(a_hi, b_lo, NT)


def moments(at, lows, coef, h0, h1, lt):
    peers, rank, rows = lows.shape
    hid = h0.shape[1]
    total, block = peers * rank, peers * rank // 2
    terms = pl.BlockSpec((2, block, hid), lambda i, at: (0, i, 0))
    specs = relative_specs(lows, 0)
    return pl.pallas_call(
        moment_kernel,
        grid_spec=pltpu.PrefetchScalarGridSpec(
            num_scalar_prefetch=1,
            grid=(2,),
            in_specs=[*specs, full_spec(coef), full_spec(h0), full_spec(h1), full_spec(lt)],
            out_specs=[terms, terms, pl.BlockSpec((block, rank), lambda i, at: (i, 0))],
        ),
        out_shape=[jax.ShapeDtypeStruct((2, total, hid), BF)] * 2 + [jax.ShapeDtypeStruct((total, rank), F32)],
        compiler_params=PARAMS,
        cost_estimate=cost(8 * total * rows * hid, 4 * total * (rows + 2 * hid) + 4 * rows * hid),
        name="moments",
    )(at, *[lows] * len(specs), coef, h0, h1, lt)


def grad_kernel(ks, at_ref, m0_ref, m1_ref, n_ref, second_ref, *refs):
    m0, m1 = (m_ref[...].reshape(-1, m_ref.shape[2]) for m_ref in (m0_ref, m1_ref))
    n_hi, n_lo = split(n_ref[...])
    outs = refs[2 * len(ks) :]
    for p, k in enumerate(ks):
        d0, d1 = as_matrix(refs[2 * p]), as_matrix(refs[2 * p + 1])
        o_hi, o_lo = split(second_ref[:, columns(at_ref, k, d0.shape[1])])
        g = mm_split(m0, d0) + mm_split(m1, d1)
        outs[0][:, p * d0.shape[1] : (p + 1) * d0.shape[1]] = g + mm(n_hi, o_hi) + mm(n_lo, o_hi) + mm(n_hi, o_lo)


def grad_sums(at, ms, n, downs, second, ks, start, total):
    hid = ms[0].shape[2]
    rank = second.shape[0]
    depth = downs[0][0][0].shape[2]
    block = min(256, total)
    row = lambda width: pl.BlockSpec((block, width), lambda i, *at: (i + start // block, 0))
    terms = pl.BlockSpec((2, block, hid), lambda i, *at: (0, i + start // block, 0))
    args, specs = [*ms, n, second], [terms, terms, row(rank), full_spec(second)]
    for k in ks:
        args += [arr for arr, _ in downs[k]]
        specs += [placed_spec(item) for item in downs[k]]
    return pl.pallas_call(
        functools.partial(grad_kernel, ks),
        grid_spec=pltpu.PrefetchScalarGridSpec(
            num_scalar_prefetch=1,
            grid=(total // block,),
            in_specs=specs,
            out_specs=pl.BlockSpec((block, len(ks) * depth), lambda i, *at: (i, 0)),
        ),
        out_shape=jax.ShapeDtypeStruct((total, len(ks) * depth), F32),
        compiler_params=PARAMS,
        cost_estimate=cost(8 * total * hid * depth * len(ks), 8 * total * hid + 4 * len(ks) * depth * (total + hid)),
        name="grad_sums",
    )(at, *args)


def key_terms(at_ref, sec_refs, d, k):
    where = columns(at_ref, k, d.shape[1]) if k is not None else slice(None)
    sec = jnp.concatenate([ref[0, :, where] for ref in sec_refs], axis=0)
    return mm_split(stacked(sec), d, NT)


def stage_kernel(ks, carry, at_ref, *refs):
    refs = list(refs)
    near_ref, far_ref, key_ref = refs[-3:]
    del refs[-3:]
    downs = refs[-len(ks) :]
    del refs[-len(ks) :]
    second_ref, n_ref, m_ref = refs[-3:]
    del refs[-3:]
    sums = [refs.pop(), refs.pop()][::-1] if carry else None
    side = pl.program_id(0)
    m = m_ref[...].reshape(-1, m_ref.shape[2])
    key = None
    parts = []
    if not carry:
        n_hi, n_lo = split(n_ref[...])
    for k, d_ref in zip(ks, downs):
        d = as_matrix(d_ref)
        term = key_terms(at_ref, refs, d, k)
        key = term if key is None else key + term
        g = mm_split(m, d)
        if not carry:
            o_hi, o_lo = split(second_ref[:, columns(at_ref, k, d.shape[1])])
            g += mm(n_hi, o_hi) + mm(n_lo, o_hi) + mm(n_hi, o_lo)
        parts.append(g)
    key_ref[...] = key
    for which, out_ref in ((0, near_ref), (1, far_ref)):

        @pl.when(side == which)
        def _():
            for p, g in enumerate(parts):
                where = slice(p * g.shape[1], (p + 1) * g.shape[1])
                out_ref[:, where] = g + sums[which][:, where] if carry else g


def down_stage(at, seconds, second, n, m, downs, ks, sums=()):
    peers, rank, width = seconds.shape
    depth = downs[0][0][0].shape[2]
    hid = downs[0][0][0].shape[1]
    total, block = peers * rank, peers * rank // 2
    row = lambda wide: pl.BlockSpec((block, wide), lambda i, at: (i, 0))
    specs = relative_specs(seconds, 0)
    items = [downs[k][0] for k in ks]
    args = [*[seconds] * len(specs), *sums, second, n, m, *(arr for arr, _ in items)]
    specs += [full_spec(v) for v in sums]
    specs += [full_spec(second), row(rank), pl.BlockSpec((2, block, hid), lambda i, at: (0, i, 0))]
    specs += [placed_spec(item) for item in items]
    part = jax.ShapeDtypeStruct((block, len(ks) * depth), F32)
    near, far, key = pl.pallas_call(
        functools.partial(stage_kernel, ks, len(sums) > 0),
        grid_spec=pltpu.PrefetchScalarGridSpec(
            num_scalar_prefetch=1, grid=(2,), in_specs=specs, out_specs=[full_spec(part), full_spec(part), row(hid)]
        ),
        out_shape=[part, part, jax.ShapeDtypeStruct((total, hid), F32)],
        compiler_params=PARAMS,
        cost_estimate=cost(8 * total * hid * len(ks) * depth, 4 * total * (width + 2 * hid)),
        name="down_stage",
    )(at, *args)
    return (near, far), key


def own_kernel(at_ref, *refs):
    *sec_refs, own_ref, s_ref = refs
    hi, lo = split(rows_of(sec_refs))
    own_hi, own_lo = split(own_ref[...])
    s_ref[...] = mm(hi, own_hi, NT) + mm(lo, own_hi, NT) + mm(hi, own_lo, NT)


def own_products(at, seconds, second):
    peers, rank, width = seconds.shape
    total, block = peers * rank, peers * rank // 2
    specs = relative_specs(seconds, 0)
    return pl.pallas_call(
        own_kernel,
        grid_spec=pltpu.PrefetchScalarGridSpec(
            num_scalar_prefetch=1,
            grid=(2,),
            in_specs=[*specs, full_spec(second)],
            out_specs=pl.BlockSpec((block, rank), lambda i, at: (i, 0)),
        ),
        out_shape=jax.ShapeDtypeStruct((total, rank), F32),
        compiler_params=PARAMS,
        cost_estimate=cost(6 * total * rank * width, 4 * total * width),
        name="own_products",
    )(at, *[seconds] * len(specs), second)


def back_kernel(at_ref, *refs):
    *sec_refs, d0_ref, d1_ref, k0_ref, k1_ref, h0_ref, h1_ref, coef_ref, s_ref, lt_ref, b_ref = refs
    b = None
    for e, d_ref, k_ref, h_ref in ((0, d0_ref, k0_ref, h0_ref), (1, d1_ref, k1_ref, h1_ref)):
        key = k_ref[...] + key_terms(at_ref, sec_refs, as_matrix(d_ref), None)
        term = mm_split(stacked(key), h_ref[...], NT) * coef_ref[e : e + 1, :]
        b = term if b is None else b + term
    s_hi, s_lo = split(s_ref[...])
    l_hi, l_lo = split(lt_ref[...])
    b_ref[...] = b + mm(s_hi, l_hi) + mm(s_lo, l_hi) + mm(s_hi, l_lo)


def back_rows(at, seconds, down, last, keys, s, h0, h1, coef, lt, side):
    hid = keys[0].shape[1]
    rows = h0.shape[0]
    rank = s.shape[1]
    block = s.shape[0] // 2
    row = lambda width: pl.BlockSpec((block, width), lambda i, at: (side, 0))
    specs = relative_specs(seconds, side, last, down[0][0].shape[2])
    args = [seconds] * len(specs)
    specs += [*(placed_spec(item) for item in down), row(hid), row(hid)]
    specs += [full_spec(h0), full_spec(h1), full_spec(coef), row(rank), full_spec(lt)]
    return pl.pallas_call(
        back_kernel,
        grid_spec=pltpu.PrefetchScalarGridSpec(
            num_scalar_prefetch=1,
            grid=(1,),
            in_specs=specs,
            out_specs=pl.BlockSpec((block, rows), lambda i, at: (0, 0)),
        ),
        out_shape=jax.ShapeDtypeStruct((block, rows), F32),
        compiler_params=PARAMS,
        cost_estimate=cost(64000 * block * rows * hid, 8000 * block * hid + 4000 * rows * hid + 4000 * block * rows),
        name="back_rows",
    )(at, *args, *(arr for arr, _ in down), *keys, h0, h1, coef, s, lt)


def swap(v, axis, mask):
    size = lax.axis_size(axis)
    return lax.ppermute(v, axis, [(i, i ^ mask) for i in range(size)])


def after(v, *done):
    return lax.optimization_barrier((v, *done))[0] if done else v


def spread(own, orders, wait=(), passing=()):
    size = lax.axis_size("dp")
    got = [[(own, p) for p in range(len(orders))]]
    for k in range(1, size):
        if k & (k - 1) == 0:
            sent = swap(after(own, *wait), "dp", k)
            got.append([(sent, p) for p in range(len(orders))])
            continue
        items = []
        for p, highest_last in enumerate(orders):
            bit = 1 << (k.bit_length() - 1) if highest_last else k & -k
            arr, place = got[k ^ bit][p]
            items.append((swap(after(arr[place : place + 1], *passing), "dp", bit), 0))
        got.append(items)
    return got


def chip_blocks(v, waits):
    got = [v]
    for m in range(1, lax.axis_size("expert") // 2):
        bit = m & -m if m & 1 else m
        got.append(swap(after(got[m ^ bit], *waits.get(m, ())), "expert", 2 * bit))
    return got


def both_cores(blocks):
    mine = jnp.stack(blocks)
    return mine, swap(mine, "expert", 1)


def chip_sums(near, far):
    got = swap(far, "expert", 1)
    half = near.shape[0] // 2
    return near[:half] + got[:half], near[half:] + got[half:]


def sum_over_chips(keep, send, dtype, waits=()):
    mask, first = 2, None
    while True:
        wait, *waits = waits or ((),)
        total = keep + swap(after(send.astype(dtype), *wait), "expert", mask).astype(F32)
        first = total if first is None else first
        half = total.shape[0] // 2
        if half == 0:
            return total[0], first
        keep, send = total[:half], total[half:]
        mask *= 2


def shares_of(index, scores, count):
    shares = scores / jnp.sum(scores, axis=1, keepdims=True)
    hit = index[:, :, None] == jnp.arange(count, dtype=jnp.int32)[None, None, :]
    return jnp.sum(jnp.where(hit, shares[:, :, None], 0.0), axis=1)


def shards(
    tokens,
    initial_expert_index,
    pruned_expert_index,
    initial_router_scores,
    pruned_router_scores,
    gate_weight,
    up_weight,
    down_weight,
    adapter_first_weight,
    adapter_second_weight,
):
    peers = lax.axis_size("expert")
    groups = lax.axis_size("dp")
    place = lax.axis_index("dp")
    me = lax.axis_index("expert")
    chips = peers // 2
    tok, width = tokens.shape
    hid = gate_weight.shape[2]
    depth = gate_weight.shape[1]
    rank = adapter_first_weight.shape[2]

    frozen = shares_of(initial_expert_index, initial_router_scores, 2 * peers).reshape(tok, peers, 2)
    kept = shares_of(pruned_expert_index, pruned_router_scores, peers)
    table = jnp.stack([kept - frozen[:, :, 0], -frozen[:, :, 1], kept], axis=2).reshape(tok, 3 * peers)
    t_hi, rest = table.astype(BF), table
    rest = rest - t_hi.astype(F32)
    t_mid = rest.astype(BF)
    t_lo = (rest - t_mid.astype(F32)).astype(BF)
    table = jnp.concatenate([t_hi, t_mid, t_lo], axis=1)
    table = jnp.pad(table, ((0, 0), (0, -table.shape[1] % LANES)))

    column = jnp.arange(table.shape[1], dtype=jnp.int32)[None, :]
    kind = jnp.arange(8, dtype=jnp.int32)[:, None]
    pick = ((column % (3 * peers) == 3 * me + kind) & (kind < 3) & (column < 9 * peers)).astype(BF)
    at = jnp.stack([me // 2, me % 2, place, me]).astype(jnp.int32)
    first_t = jnp.concatenate(split(adapter_first_weight[0].T), axis=0)
    second = adapter_second_weight[0]

    last = groups - 1
    most = list(range(last))
    def direct(got):
        return [got[1 << p][0][0] for p in range(groups.bit_length() - 1)]

    def ends(got):
        return [arr for arr, _ in got[last]]

    def both(first, second):
        return [a + b for a, b in zip(first, second)]

    def with_own(got, *own):
        return [list(own)] + got[1:]

    pair0 = spread(jnp.stack([gate_weight[0], up_weight[0]]), (True, False))
    w0 = with_own(pair0, (gate_weight, 0), (up_weight, 0))

    packet = jnp.concatenate([tokens, table], axis=1)
    x = lax.all_gather(packet, "expert", axis=0, tiled=True)
    seconds = lax.all_gather(after(second, *direct(pair0)), "expert", axis=0)
    h0, lt, coef = hidden_rows(at, x, w0, most + [last], (), True, first_t, pick)

    gate1 = spread(gate_weight[1:2], (True,), ends(pair0))
    up1 = spread(up_weight[1:2], (False,), ends(pair0))
    w1 = with_own(both(gate1, up1), (gate_weight, 1), (up_weight, 1))
    direct1 = direct(gate1) + direct(up1)
    lows = lax.all_gather(after(lt, *direct1, seconds), "expert", axis=0)
    (h1,) = hidden_rows(at, x, w1, most + [last])
    down0 = spread(down_weight[0:1], (True,), ends(gate1) + ends(up1))
    own0 = with_own(down0, (down_weight, 0))
    *ms, n = moments(at, lows, coef, h0, h1, lt)
    parts, key0 = down_stage(at, seconds, second, n, ms[0], own0, most)
    down1 = spread(down_weight[1:2], (False,), (h1, *direct(down0)), (key0,))
    own1 = with_own(down1, (down_weight, 1))

    def blocks(v):
        return v.reshape(chips, rank, -1)

    s = own_products(at, after(seconds, h1), second)
    parts, key1 = down_stage(at, seconds, second, n, ms[1], own1, most, parts)
    downs = both(own0, own1)

    def back(side, *wait):
        return blocks(back_rows(at, seconds, downs[last], last, (key0, key1), s, h0, h1, after(coef, *wait), lt, side))

    far = back(1)
    far = back(1)
    near_early, far_early = (blocks(part) for part in parts)
    early = chip_sums(near_early, far_early)
    near = back(0, far, early[1])
    sums = chip_sums(near, far)
    b, b_first = sum_over_chips(*sums, F32)
    b = b * coef[2:3, :]
    early, early_first = sum_over_chips(*early, BF)
    late = chip_sums(
        *(
            blocks(grad_sums(at, [after(ms[0], sums[1]), ms[1]], n, downs, second, [last], start, chips * rank))
            for start in (0, chips * rank)
        )
    )
    late, _ = sum_over_chips(*late, BF, ((early_first,),))

    over_tokens = (((0,), (1,)), ((), ()))
    b_hi, b_lo = split(b)
    part_a = mm(h0, b_hi, over_tokens) + mm(h0, b_lo, over_tokens)
    rows = hid // groups
    grad_a = lax.dynamic_slice_in_dim(part_a, place * rows, rows, 0)
    for k in range(1, groups):
        grad_a = grad_a + swap(lax.dynamic_slice_in_dim(part_a, (place ^ k) * rows, rows, 0), "dp", k)
    grad_b = early[:, :depth]
    for k in range(1, groups):
        part = late if k == last else early[:, k * depth : (k + 1) * depth]
        grad_b = grad_b + swap(part, "dp", k)
    return grad_a[None], grad_b[None]


def solution(mesh):
    placed = (
        P(("dp", "expert"), None),
        P(("dp", "expert"), None),
        P(("dp", "expert"), None),
        P(("dp", "expert"), None),
        P(("dp", "expert"), None),
        P("expert", "dp", None),
        P("expert", "dp", None),
        P("expert", None, "dp"),
        P("expert", None, None),
        P("expert", None, None),
    )
    return jax.shard_map(
        shards,
        mesh=mesh,
        in_specs=placed,
        out_specs=(P("expert", "dp", None), P("expert", None, "dp")),
        check_vma=False,
    )
```

```python
import functools

import jax
import jax.numpy as jnp
from jax import lax
from jax.experimental import pallas as pl
from jax.experimental.pallas import tpu as pltpu
from jax.sharding import PartitionSpec as P

BF = jnp.bfloat16
F32 = jnp.float32
LANES = 128
NN = (((1,), (0,)), ((), ()))
NT = (((1,), (1,)), ((), ()))
PARAMS = pltpu.CompilerParams(vmem_limit_bytes=48 * 1024 * 1024)


def mm(a, b, dims=NN):
    return lax.dot_general(a, b, dims, preferred_element_type=F32)


def mm_full(a, b, dims=NN):
    return lax.dot_general(a, b, dims, precision=lax.Precision.HIGHEST, preferred_element_type=F32)


def split(v):
    hi = v.astype(BF)
    return hi, (v - hi.astype(F32)).astype(BF)


def stacked(v):
    return jnp.concatenate(split(v), axis=0)


def mm_split(a, b, dims=NN):
    both = mm(a, b, dims)
    half = a.shape[0] // 2
    return both[:half] + both[half:]


def cost(flops, nbytes):
    return pl.CostEstimate(flops=flops // 1000, bytes_accessed=nbytes // 1000, transcendentals=0)


def full_spec(a):
    zeros = (0,) * a.ndim
    return pl.BlockSpec(a.shape, lambda i, *at: zeros)


def table_columns(peers):
    column = jnp.arange(-(-9 * peers // LANES) * LANES, dtype=jnp.int32)
    kind = column % 3
    pair = column % (3 * peers) // 3
    used = column < 9 * peers
    frozen = jnp.where(used & (kind < 2), 2 * pair + kind, -1)
    kept = jnp.where(used & (kind != 1), pair, -1)
    return jnp.stack([frozen, kept, column // (3 * peers)]).astype(F32)


def packet_kernel(top, tokens_ref, routes_ref, columns_ref, x_ref):
    width = tokens_ref.shape[1]
    x_ref[:, :width] = tokens_ref[...]
    routes = routes_ref[...].T
    frozen_index, kept_index, frozen, kept = (routes[:, i * top : (i + 1) * top] for i in range(4))
    frozen, kept = (v / jnp.sum(v, axis=1, keepdims=True) for v in (frozen, kept))
    value = jnp.zeros((tokens_ref.shape[0], columns_ref.shape[1]), F32)
    for k in range(top):
        value += jnp.where(kept_index[:, k : k + 1] == columns_ref[1:2, :], kept[:, k : k + 1], 0.0)
        value -= jnp.where(frozen_index[:, k : k + 1] == columns_ref[0:1, :], frozen[:, k : k + 1], 0.0)
    hi = value.astype(BF).astype(F32)
    mid = (value - hi).astype(BF).astype(F32)
    term = columns_ref[2:3, :]
    x_ref[:, width:] = jnp.where(term == 0.0, hi, jnp.where(term == 1.0, mid, value - hi - mid)).astype(BF)


def packets(tokens, frozen_index, kept_index, frozen, kept, columns):
    tok, width = tokens.shape
    top = frozen.shape[1]
    routes = jnp.concatenate([frozen_index.T.astype(F32), kept_index.T.astype(F32), frozen.T, kept.T], axis=0)
    args = [tokens, routes, columns]
    out_shape = jax.ShapeDtypeStruct((tok, width + columns.shape[1]), BF)
    return pl.pallas_call(
        functools.partial(packet_kernel, top),
        grid=(1,),
        in_specs=[full_spec(v) for v in args],
        out_specs=full_spec(out_shape),
        out_shape=out_shape,
        compiler_params=PARAMS,
        cost_estimate=cost(0, 0),
        name="packets",
    )(*args)


def copy_kernel(*refs):
    half = len(refs) // 2
    for source, target in zip(refs[:half], refs[half:]):
        target[...] = source[...]


def own_slices(*items):
    out_shape = [jax.ShapeDtypeStruct((1, *arr.shape[1:]), arr.dtype) for arr, _ in items]
    return pl.pallas_call(
        copy_kernel,
        grid=(1,),
        in_specs=[placed_spec(item) for item in items],
        out_specs=[full_spec(v) for v in out_shape],
        out_shape=out_shape,
        compiler_params=PARAMS,
        cost_estimate=cost(0, 0),
        name="own_slices",
    )(*(arr for arr, _ in items))


def columns(at_ref, k, depth):
    return pl.ds(pl.multiple_of((at_ref[2] ^ k) * depth, LANES), depth)


def as_matrix(ref):
    return ref[...].reshape(ref.shape[-2:])


def halving(chips):
    order = [0]
    while len(order) < chips:
        order = [2 * m for m in order] + [2 * m + 1 for m in order]
    return order


def relative_specs(blocks, start, k=None, depth=None):
    def spec(m):
        if k is not None:
            return pl.BlockSpec(
                (1, blocks.shape[1], depth), lambda i, at: (at[3] ^ (2 * m + i + start), 0, at[2] ^ k)
            )
        return pl.BlockSpec((1, *blocks.shape[1:]), lambda i, at: (at[3] ^ (2 * m + i + start), 0, 0))

    return [spec(m) for m in halving(blocks.shape[0] // 2)]


def rows_of(refs):
    return jnp.concatenate([ref[0] for ref in refs], axis=0)


def placed_spec(item):
    arr, index = item
    return pl.BlockSpec((1, *arr.shape[1:]), lambda *_: (index, 0, 0))


def hidden_kernel(ks, carry, finish, low, at_ref, x_ref, *refs):
    refs = list(refs)
    gates = [refs.pop(0) for _ in ks]
    ups = [refs.pop(0) for _ in ks]
    gate, up = (refs.pop(0)[...], refs.pop(0)[...]) if carry else (None, None)
    depth = gates[0].shape[1]
    for k, g_ref, u_ref in zip(ks, gates, ups):
        x = x_ref[:, columns(at_ref, k, depth)] if x_ref.shape[1] > depth else x_ref[...]
        g = mm(x, as_matrix(g_ref))
        u = mm(x, as_matrix(u_ref))
        gate = g if gate is None else gate + g
        up = u if up is None else up + u
    if not finish:
        gate_ref, up_ref = refs
        gate_ref[...] = gate
        up_ref[...] = up
        return
    hidden = (gate / (1.0 + jnp.exp(-gate)) * up).astype(BF)
    if low:
        first_ref, pick_ref, h_ref, lt_ref, coef_ref = refs
        rank = lt_ref.shape[0]
        coef = mm(pick_ref[...], x_ref[:, x_ref.shape[1] - pick_ref.shape[1] :], NT)
        both = mm(first_ref[...], hidden, NT)
        lt_ref[...] = (both[:rank] + both[rank:]) * coef[2:3, :]
        coef_ref[...] = coef
    else:
        (h_ref,) = refs
    h_ref[...] = hidden


def hidden_rows(at, x, items, ks, sums=(), finish=True, first_t=None, pick=None):
    rows, wide = x.shape
    depth, hid = items[0][0][0].shape[1:]
    block = min(256, rows)
    items = [items[k][p] for p in range(2) for k in ks]
    if len(ks) == 1:
        specs = [pl.BlockSpec((block, depth), lambda i, at: (i, at[2] ^ ks[0]))]
        wide = depth
    else:
        specs = [pl.BlockSpec((block, wide), lambda i, at: (i, 0))]
    specs += [placed_spec(item) for item in items]
    row = pl.BlockSpec((block, hid), lambda i, at: (i, 0))
    specs += [row] * len(sums)
    args = [x, *(arr for arr, _ in items), *sums]
    if not finish:
        out_shape = [jax.ShapeDtypeStruct((rows, hid), F32)] * 2
        out_specs = [row, row]
    else:
        out_shape = [jax.ShapeDtypeStruct((rows, hid), BF)]
        out_specs = [row]
    if first_t is not None:
        args += [first_t, pick]
        specs += [full_spec(first_t), full_spec(pick)]
        for count in (first_t.shape[0] // 2, pick.shape[0]):
            out_shape.append(jax.ShapeDtypeStruct((count, rows), F32))
            out_specs.append(pl.BlockSpec((count, block), lambda i, at: (0, i)))
    return pl.pallas_call(
        functools.partial(hidden_kernel, ks, len(sums) > 0, finish, first_t is not None),
        grid_spec=pltpu.PrefetchScalarGridSpec(
            num_scalar_prefetch=1,
            grid=(rows // block,),
            in_specs=specs,
            out_specs=out_specs,
        ),
        out_shape=out_shape,
        compiler_params=PARAMS,
        cost_estimate=cost(4 * rows * depth * len(ks) * hid, rows * (2 * wide + 2 * hid) + 4 * depth * len(ks) * hid),
        name="hidden_rows",
    )(at, *args)


def moment_kernel(at_ref, *refs):
    coef_ref, h0_ref, h1_ref, own_ref, m0_ref, m1_ref, n_ref = refs[-7:]
    lt = rows_of(refs[:-7])
    for which, h_ref, m_ref in ((0, h0_ref, m0_ref), (1, h1_ref, m1_ref)):
        hi, lo = split(mm_split(stacked(lt * coef_ref[which : which + 1, :]), h_ref[...]))
        m_ref[0] = hi
        m_ref[1] = lo
    a_hi, a_lo = split(lt)
    b_hi, b_lo = split(own_ref[...])
    n_ref[...] = mm(a_hi, b_hi, NT) + mm(a_lo, b_hi, NT) + mm(a_hi, b_lo, NT)


def moments(at, lows, coef, h0, h1, lt):
    peers, rank, rows = lows.shape
    hid = h0.shape[1]
    total, block = peers * rank, peers * rank // 2
    terms = pl.BlockSpec((2, block, hid), lambda i, at: (0, i, 0))
    specs = relative_specs(lows, 0)
    return pl.pallas_call(
        moment_kernel,
        grid_spec=pltpu.PrefetchScalarGridSpec(
            num_scalar_prefetch=1,
            grid=(2,),
            in_specs=[*specs, full_spec(coef), full_spec(h0), full_spec(h1), full_spec(lt)],
            out_specs=[terms, terms, pl.BlockSpec((block, rank), lambda i, at: (i, 0))],
        ),
        out_shape=[jax.ShapeDtypeStruct((2, total, hid), BF)] * 2 + [jax.ShapeDtypeStruct((total, rank), F32)],
        compiler_params=PARAMS,
        cost_estimate=cost(8 * total * rows * hid, 4 * total * (rows + 2 * hid) + 4 * rows * hid),
        name="moments",
    )(at, *[lows] * len(specs), coef, h0, h1, lt)


def grad_kernel(ks, at_ref, m0_ref, m1_ref, n_ref, second_ref, *refs):
    m0, m1 = (m_ref[...].reshape(-1, m_ref.shape[2]) for m_ref in (m0_ref, m1_ref))
    n_hi, n_lo = split(n_ref[...])
    outs = refs[2 * len(ks) :]
    for p, k in enumerate(ks):
        d0, d1 = as_matrix(refs[2 * p]), as_matrix(refs[2 * p + 1])
        o_hi, o_lo = split(second_ref[:, columns(at_ref, k, d0.shape[1])])
        g = mm_split(m0, d0) + mm_split(m1, d1)
        outs[0][:, p * d0.shape[1] : (p + 1) * d0.shape[1]] = g + mm(n_hi, o_hi) + mm(n_lo, o_hi) + mm(n_hi, o_lo)


def grad_sums(at, ms, n, downs, second, ks, start, total):
    hid = ms[0].shape[2]
    rank = second.shape[0]
    depth = downs[0][0][0].shape[2]
    block = min(256, total)
    row = lambda width: pl.BlockSpec((block, width), lambda i, *at: (i + start // block, 0))
    terms = pl.BlockSpec((2, block, hid), lambda i, *at: (0, i + start // block, 0))
    args, specs = [*ms, n, second], [terms, terms, row(rank), full_spec(second)]
    for k in ks:
        args += [arr for arr, _ in downs[k]]
        specs += [placed_spec(item) for item in downs[k]]
    return pl.pallas_call(
        functools.partial(grad_kernel, ks),
        grid_spec=pltpu.PrefetchScalarGridSpec(
            num_scalar_prefetch=1,
            grid=(total // block,),
            in_specs=specs,
            out_specs=pl.BlockSpec((block, len(ks) * depth), lambda i, *at: (i, 0)),
        ),
        out_shape=jax.ShapeDtypeStruct((total, len(ks) * depth), F32),
        compiler_params=PARAMS,
        cost_estimate=cost(8 * total * hid * depth * len(ks), 8 * total * hid + 4 * len(ks) * depth * (total + hid)),
        name="grad_sums",
    )(at, *args)


def key_terms(at_ref, sec_refs, d, k):
    where = columns(at_ref, k, d.shape[1]) if k is not None else slice(None)
    sec = jnp.concatenate([ref[0, :, where] for ref in sec_refs], axis=0)
    return mm_split(stacked(sec), d, NT)


def stage_kernel(ks, carry, at_ref, *refs):
    refs = list(refs)
    near_ref, far_ref, key_ref = refs[-3:]
    del refs[-3:]
    downs = refs[-len(ks) :]
    del refs[-len(ks) :]
    second_ref, n_ref, m_ref = refs[-3:]
    del refs[-3:]
    sums = [refs.pop(), refs.pop()][::-1] if carry else None
    side = pl.program_id(0)
    m = m_ref[...].reshape(-1, m_ref.shape[2])
    key = None
    parts = []
    if not carry:
        n_hi, n_lo = split(n_ref[...])
    for k, d_ref in zip(ks, downs):
        d = as_matrix(d_ref)
        term = key_terms(at_ref, refs, d, k)
        key = term if key is None else key + term
        g = mm_split(m, d)
        if not carry:
            o_hi, o_lo = split(second_ref[:, columns(at_ref, k, d.shape[1])])
            g += mm(n_hi, o_hi) + mm(n_lo, o_hi) + mm(n_hi, o_lo)
        parts.append(g)
    key_ref[...] = key
    for which, out_ref in ((0, near_ref), (1, far_ref)):

        @pl.when(side == which)
        def _():
            for p, g in enumerate(parts):
                where = slice(p * g.shape[1], (p + 1) * g.shape[1])
                out_ref[:, where] = g + sums[which][:, where] if carry else g


def down_stage(at, seconds, second, n, m, downs, ks, sums=()):
    peers, rank, width = seconds.shape
    depth = downs[0][0][0].shape[2]
    hid = downs[0][0][0].shape[1]
    total, block = peers * rank, peers * rank // 2
    row = lambda wide: pl.BlockSpec((block, wide), lambda i, at: (i, 0))
    specs = relative_specs(seconds, 0)
    items = [downs[k][0] for k in ks]
    args = [*[seconds] * len(specs), *sums, second, n, m, *(arr for arr, _ in items)]
    specs += [full_spec(v) for v in sums]
    specs += [full_spec(second), row(rank), pl.BlockSpec((2, block, hid), lambda i, at: (0, i, 0))]
    specs += [placed_spec(item) for item in items]
    part = jax.ShapeDtypeStruct((block, len(ks) * depth), F32)
    near, far, key = pl.pallas_call(
        functools.partial(stage_kernel, ks, len(sums) > 0),
        grid_spec=pltpu.PrefetchScalarGridSpec(
            num_scalar_prefetch=1, grid=(2,), in_specs=specs, out_specs=[full_spec(part), full_spec(part), row(hid)]
        ),
        out_shape=[part, part, jax.ShapeDtypeStruct((total, hid), F32)],
        compiler_params=PARAMS,
        cost_estimate=cost(8 * total * hid * len(ks) * depth, 4 * total * (width + 2 * hid)),
        name="down_stage",
    )(at, *args)
    return (near, far), key


def own_kernel(at_ref, *refs):
    *sec_refs, own_ref, s_ref = refs
    hi, lo = split(rows_of(sec_refs))
    own_hi, own_lo = split(own_ref[...])
    s_ref[...] = mm(hi, own_hi, NT) + mm(lo, own_hi, NT) + mm(hi, own_lo, NT)


def own_products(at, seconds, second):
    peers, rank, width = seconds.shape
    total, block = peers * rank, peers * rank // 2
    specs = relative_specs(seconds, 0)
    return pl.pallas_call(
        own_kernel,
        grid_spec=pltpu.PrefetchScalarGridSpec(
            num_scalar_prefetch=1,
            grid=(2,),
            in_specs=[*specs, full_spec(second)],
            out_specs=pl.BlockSpec((block, rank), lambda i, at: (i, 0)),
        ),
        out_shape=jax.ShapeDtypeStruct((total, rank), F32),
        compiler_params=PARAMS,
        cost_estimate=cost(6 * total * rank * width, 4 * total * width),
        name="own_products",
    )(at, *[seconds] * len(specs), second)


def back_kernel(at_ref, *refs):
    *sec_refs, d0_ref, d1_ref, k0_ref, k1_ref, h0_ref, h1_ref, coef_ref, s_ref, lt_ref, b_ref = refs
    b = None
    for e, d_ref, k_ref, h_ref in ((0, d0_ref, k0_ref, h0_ref), (1, d1_ref, k1_ref, h1_ref)):
        key = k_ref[...] + key_terms(at_ref, sec_refs, as_matrix(d_ref), None)
        term = mm_split(stacked(key), h_ref[...], NT) * coef_ref[e : e + 1, :]
        b = term if b is None else b + term
    s_hi, s_lo = split(s_ref[...])
    l_hi, l_lo = split(lt_ref[...])
    b_ref[...] = b + mm(s_hi, l_hi) + mm(s_lo, l_hi) + mm(s_hi, l_lo)


def back_rows(at, seconds, down, last, keys, s, h0, h1, coef, lt, side):
    hid = keys[0].shape[1]
    rows = h0.shape[0]
    rank = s.shape[1]
    block = s.shape[0] // 2
    row = lambda width: pl.BlockSpec((block, width), lambda i, at: (side, 0))
    specs = relative_specs(seconds, side, last, down[0][0].shape[2])
    args = [seconds] * len(specs)
    specs += [*(placed_spec(item) for item in down), row(hid), row(hid)]
    specs += [full_spec(h0), full_spec(h1), full_spec(coef), row(rank), full_spec(lt)]
    return pl.pallas_call(
        back_kernel,
        grid_spec=pltpu.PrefetchScalarGridSpec(
            num_scalar_prefetch=1,
            grid=(1,),
            in_specs=specs,
            out_specs=pl.BlockSpec((block, rows), lambda i, at: (0, 0)),
        ),
        out_shape=jax.ShapeDtypeStruct((block, rows), F32),
        compiler_params=PARAMS,
        cost_estimate=cost(64000 * block * rows * hid, 8000 * block * hid + 4000 * rows * hid + 4000 * block * rows),
        name="back_rows",
    )(at, *args, *(arr for arr, _ in down), *keys, h0, h1, coef, s, lt)


def swap(v, axis, mask):
    size = lax.axis_size(axis)
    return lax.ppermute(v, axis, [(i, i ^ mask) for i in range(size)])


def after(v, *done):
    return lax.optimization_barrier((v, *done))[0] if done else v


def spread(own, orders, wait=(), passing=()):
    size = lax.axis_size("dp")
    got = [[(own, p) for p in range(len(orders))]]
    for k in range(1, size):
        if k & (k - 1) == 0:
            sent = swap(after(own, *wait), "dp", k)
            got.append([(sent, p) for p in range(len(orders))])
            continue
        items = []
        for p, highest_last in enumerate(orders):
            bit = 1 << (k.bit_length() - 1) if highest_last else k & -k
            arr, place = got[k ^ bit][p]
            items.append((swap(after(arr[place : place + 1], *passing), "dp", bit), 0))
        got.append(items)
    return got


def chip_blocks(v, waits):
    got = [v]
    for m in range(1, lax.axis_size("expert") // 2):
        bit = m & -m if m & 1 else m
        got.append(swap(after(got[m ^ bit], *waits.get(m, ())), "expert", 2 * bit))
    return got


def both_cores(blocks):
    mine = jnp.stack(blocks)
    return mine, swap(mine, "expert", 1)


def chip_sums(near, far):
    got = swap(far, "expert", 1)
    half = near.shape[0] // 2
    return near[:half] + got[:half], near[half:] + got[half:]


def sum_over_chips(keep, send, dtype, waits=()):
    mask, first = 2, None
    while True:
        wait, *waits = waits or ((),)
        total = keep + swap(after(send.astype(dtype), *wait), "expert", mask).astype(F32)
        first = total if first is None else first
        half = total.shape[0] // 2
        if half == 0:
            return total[0], first
        keep, send = total[:half], total[half:]
        mask *= 2


def shards(
    tokens,
    initial_expert_index,
    pruned_expert_index,
    initial_router_scores,
    pruned_router_scores,
    gate_weight,
    up_weight,
    down_weight,
    adapter_first_weight,
    adapter_second_weight,
):
    peers = lax.axis_size("expert")
    groups = lax.axis_size("dp")
    place = lax.axis_index("dp")
    me = lax.axis_index("expert")
    chips = peers // 2
    tok, width = tokens.shape
    hid = gate_weight.shape[2]
    depth = gate_weight.shape[1]
    rank = adapter_first_weight.shape[2]

    chosen = table_columns(peers)
    kind = jnp.arange(8, dtype=jnp.int32)[:, None]
    column = jnp.arange(chosen.shape[1], dtype=jnp.int32)[None, :]
    pick = ((column % (3 * peers) == 3 * me + kind) & (kind < 3) & (column < 9 * peers)).astype(BF)
    at = jnp.stack([me // 2, me % 2, place, me]).astype(jnp.int32)
    first_t = jnp.concatenate(split(adapter_first_weight[0].T), axis=0)
    second = adapter_second_weight[0]

    last = groups - 1
    most = list(range(last))
    def direct(got):
        return [got[1 << p][0][0] for p in range(groups.bit_length() - 1)]

    def ends(got):
        return [arr for arr, _ in got[last]]

    def both(first, second):
        return [a + b for a, b in zip(first, second)]

    packet = packets(
        tokens, initial_expert_index, pruned_expert_index, initial_router_scores, pruned_router_scores, chosen
    )
    own_gate0, own_up0 = gate_weight[0:1], up_weight[0:1]
    own_gate1, own_up1, own_down0, own_down1 = own_slices(
        (gate_weight, 1), (up_weight, 1), (down_weight, 0), (down_weight, 1)
    )
    gate0 = spread(own_gate0, (True,))
    up0 = spread(own_up0, (False,))
    w0 = both(gate0, up0)
    x = lax.all_gather(packet, "expert", axis=0, tiled=True)
    seconds = lax.all_gather(after(second, *direct(gate0), *direct(up0), own_gate1), "expert", axis=0)
    h0, lt, coef = hidden_rows(at, x, w0, most + [last], (), True, first_t, pick)

    gate1 = spread(own_gate1, (True,), direct(up0))
    up1 = spread(own_up1, (False,), ends(gate0) + ends(up0))
    w1 = both(gate1, up1)
    direct1 = direct(gate1) + direct(up1)
    lows = lax.all_gather(after(lt, *direct1), "expert", axis=0)
    s = own_products(at, seconds, second)
    (h1,) = hidden_rows(at, after(x, s), w1, most + [last])
    down0 = spread(own_down0, (True,), (*ends(gate1), *ends(up1), s))
    *ms, n = moments(at, lows, coef, h0, h1, lt)
    parts, key0 = down_stage(at, seconds, second, n, ms[0], down0, most)
    down1 = spread(own_down1, (False,), (h1,), (key0,))

    def blocks(v):
        return v.reshape(chips, rank, -1)

    parts, key1 = down_stage(at, seconds, second, n, ms[1], down1, most, parts)
    downs = both(down0, down1)

    def back(side, *wait):
        return blocks(back_rows(at, seconds, downs[last], last, (key0, key1), s, h0, h1, after(coef, *wait), lt, side))

    far = back(1)
    far = back(1)
    near_early, far_early = (blocks(part) for part in parts)
    early = chip_sums(near_early, far_early)
    near = back(0, far, early[1])
    sums = chip_sums(near, far)
    b, b_first = sum_over_chips(*sums, BF)
    b = b * coef[2:3, :]
    early, early_first = sum_over_chips(*early, BF)
    late = chip_sums(
        *(
            blocks(grad_sums(at, [after(ms[0], sums[1]), ms[1]], n, downs, second, [last], start, chips * rank))
            for start in (0, chips * rank)
        )
    )
    late, _ = sum_over_chips(*late, BF, ((early_first,),))

    over_tokens = (((0,), (1,)), ((), ()))
    b_hi, b_lo = split(b)
    part_a = mm(h0, b_hi, over_tokens) + mm(h0, b_lo, over_tokens)
    rows = hid // groups
    grad_a = lax.dynamic_slice_in_dim(part_a, place * rows, rows, 0)
    for k in range(1, groups):
        grad_a = grad_a + swap(lax.dynamic_slice_in_dim(part_a, (place ^ k) * rows, rows, 0), "dp", k)
    grad_b = early[:, :depth]
    for k in range(1, groups):
        part = late if k == last else early[:, k * depth : (k + 1) * depth]
        grad_b = grad_b + swap(after(part, b_first), "dp", k)
    return grad_a[None], grad_b[None]


def solution(mesh):
    placed = (
        P(("dp", "expert"), None),
        P(("dp", "expert"), None),
        P(("dp", "expert"), None),
        P(("dp", "expert"), None),
        P(("dp", "expert"), None),
        P("expert", "dp", None),
        P("expert", "dp", None),
        P("expert", None, "dp"),
        P("expert", None, None),
        P("expert", None, None),
    )
    return jax.shard_map(
        shards,
        mesh=mesh,
        in_specs=placed,
        out_specs=(P("expert", "dp", None), P("expert", None, "dp")),
        check_vma=False,
    )
```

```python
import functools

import jax
import jax.numpy as jnp
from jax import lax
from jax.experimental import pallas as pl
from jax.experimental.pallas import tpu as pltpu
from jax.sharding import PartitionSpec as P

BF = jnp.bfloat16
F32 = jnp.float32
LANES = 128
NN = (((1,), (0,)), ((), ()))
NT = (((1,), (1,)), ((), ()))
PARAMS = pltpu.CompilerParams(vmem_limit_bytes=48 * 1024 * 1024)


def mm(a, b, dims=NN):
    return lax.dot_general(a, b, dims, preferred_element_type=F32)


def split(v):
    hi = v.astype(BF)
    return hi, (v - hi.astype(F32)).astype(BF)


def stacked(v):
    return jnp.concatenate(split(v), axis=0)


def mm_split(a, b, dims=NN):
    both = mm(a, b, dims)
    half = a.shape[0] // 2
    return both[:half] + both[half:]


def mm_full(a, b):
    a_hi, a_lo = split(a)
    b_hi, b_lo = split(b)
    return mm(jnp.concatenate([a_hi, a_lo, a_hi], axis=1), jnp.concatenate([b_hi, b_hi, b_lo], axis=0))


def cost(flops, nbytes):
    return pl.CostEstimate(flops=flops // 1000, bytes_accessed=nbytes // 1000, transcendentals=0)


def full_spec(a):
    zeros = (0,) * a.ndim
    return pl.BlockSpec(a.shape, lambda i, *at: zeros)


def table_columns(peers):
    column = jnp.arange(-(-9 * peers // LANES) * LANES, dtype=jnp.int32)
    kind = column % 3
    pair = column % (3 * peers) // 3
    used = column < 9 * peers
    frozen = jnp.where(used & (kind < 2), 2 * pair + kind, -1)
    kept = jnp.where(used & (kind != 1), pair, -1)
    return jnp.stack([frozen, kept, column // (3 * peers)]).astype(F32)


def packet_kernel(top, tokens_ref, routes_ref, columns_ref, x_ref):
    width = tokens_ref.shape[1]
    x_ref[:, :width] = tokens_ref[...]
    routes = routes_ref[...].T
    frozen_index, kept_index, frozen, kept = (routes[:, i * top : (i + 1) * top] for i in range(4))
    frozen, kept = (v / jnp.sum(v, axis=1, keepdims=True) for v in (frozen, kept))
    value = jnp.zeros((tokens_ref.shape[0], columns_ref.shape[1]), F32)
    for k in range(top):
        value += jnp.where(kept_index[:, k : k + 1] == columns_ref[1:2, :], kept[:, k : k + 1], 0.0)
        value -= jnp.where(frozen_index[:, k : k + 1] == columns_ref[0:1, :], frozen[:, k : k + 1], 0.0)
    hi = value.astype(BF).astype(F32)
    mid = (value - hi).astype(BF).astype(F32)
    term = columns_ref[2:3, :]
    x_ref[:, width:] = jnp.where(term == 0.0, hi, jnp.where(term == 1.0, mid, value - hi - mid)).astype(BF)


def packets(tokens, frozen_index, kept_index, frozen, kept, columns):
    tok, width = tokens.shape
    top = frozen.shape[1]
    routes = jnp.concatenate([frozen_index.T.astype(F32), kept_index.T.astype(F32), frozen.T, kept.T], axis=0)
    args = [tokens, routes, columns]
    out_shape = jax.ShapeDtypeStruct((tok, width + columns.shape[1]), BF)
    return pl.pallas_call(
        functools.partial(packet_kernel, top),
        grid=(1,),
        in_specs=[full_spec(v) for v in args],
        out_specs=full_spec(out_shape),
        out_shape=out_shape,
        compiler_params=PARAMS,
        cost_estimate=cost(0, 0),
        name="packets",
    )(*args)


def copy_kernel(*refs):
    half = len(refs) // 2
    for source, target in zip(refs[:half], refs[half:]):
        target[...] = source[...]


def own_slices(*items):
    out_shape = [jax.ShapeDtypeStruct((1, *arr.shape[1:]), arr.dtype) for arr, _ in items]
    return pl.pallas_call(
        copy_kernel,
        grid=(1,),
        in_specs=[placed_spec(item) for item in items],
        out_specs=[full_spec(v) for v in out_shape],
        out_shape=out_shape,
        compiler_params=PARAMS,
        cost_estimate=cost(0, 0),
        name="own_slices",
    )(*(arr for arr, _ in items))


def columns(at_ref, k, depth):
    return pl.ds(pl.multiple_of((at_ref[2] ^ k) * depth, LANES), depth)


def as_matrix(ref):
    return ref[...].reshape(ref.shape[-2:])


def halving(chips):
    order = [0]
    while len(order) < chips:
        order = [2 * m for m in order] + [2 * m + 1 for m in order]
    return order


def relative_specs(blocks, start, k=None, depth=None):
    def spec(m):
        if k is not None:
            return pl.BlockSpec(
                (1, blocks.shape[1], depth), lambda i, at: (at[3] ^ (2 * m + i + start), 0, at[2] ^ k)
            )
        return pl.BlockSpec((1, *blocks.shape[1:]), lambda i, at: (at[3] ^ (2 * m + i + start), 0, 0))

    return [spec(m) for m in halving(blocks.shape[0] // 2)]


def rows_of(refs):
    return jnp.concatenate([ref[0] for ref in refs], axis=0)


def placed_spec(item):
    arr, index = item
    return pl.BlockSpec((1, *arr.shape[1:]), lambda *_: (index, 0, 0))


def hidden_kernel(ks, carry, finish, low, at_ref, x_ref, *refs):
    refs = list(refs)
    gates = [refs.pop(0) for _ in ks]
    ups = [refs.pop(0) for _ in ks]
    gate, up = (refs.pop(0)[...], refs.pop(0)[...]) if carry else (None, None)
    depth = gates[0].shape[1]
    for k, g_ref, u_ref in zip(ks, gates, ups):
        x = x_ref[:, columns(at_ref, k, depth)] if x_ref.shape[1] > depth else x_ref[...]
        g = mm(x, as_matrix(g_ref))
        u = mm(x, as_matrix(u_ref))
        gate = g if gate is None else gate + g
        up = u if up is None else up + u
    if not finish:
        gate_ref, up_ref = refs
        gate_ref[...] = gate
        up_ref[...] = up
        return
    hidden = (gate / (1.0 + jnp.exp(-gate)) * up).astype(BF)
    if low:
        first_ref, pick_ref, h_ref, lt_ref, coef_ref = refs
        rank = lt_ref.shape[0]
        coef = mm(pick_ref[...], x_ref[:, x_ref.shape[1] - pick_ref.shape[1] :], NT)
        both = mm(first_ref[...], hidden, NT)
        lt_ref[...] = (both[:rank] + both[rank:]) * coef[2:3, :]
        coef_ref[...] = coef
    else:
        (h_ref,) = refs
    h_ref[...] = hidden


def hidden_rows(at, x, items, ks, sums=(), finish=True, first_t=None, pick=None):
    rows, wide = x.shape
    depth, hid = items[0][0][0].shape[1:]
    block = min(256, rows)
    items = [items[k][p] for p in range(2) for k in ks]
    if len(ks) == 1:
        specs = [pl.BlockSpec((block, depth), lambda i, at: (i, at[2] ^ ks[0]))]
        wide = depth
    else:
        specs = [pl.BlockSpec((block, wide), lambda i, at: (i, 0))]
    specs += [placed_spec(item) for item in items]
    row = pl.BlockSpec((block, hid), lambda i, at: (i, 0))
    specs += [row] * len(sums)
    args = [x, *(arr for arr, _ in items), *sums]
    if not finish:
        out_shape = [jax.ShapeDtypeStruct((rows, hid), F32)] * 2
        out_specs = [row, row]
    else:
        out_shape = [jax.ShapeDtypeStruct((rows, hid), BF)]
        out_specs = [row]
    if first_t is not None:
        args += [first_t, pick]
        specs += [full_spec(first_t), full_spec(pick)]
        for count in (first_t.shape[0] // 2, pick.shape[0]):
            out_shape.append(jax.ShapeDtypeStruct((count, rows), F32))
            out_specs.append(pl.BlockSpec((count, block), lambda i, at: (0, i)))
    return pl.pallas_call(
        functools.partial(hidden_kernel, ks, len(sums) > 0, finish, first_t is not None),
        grid_spec=pltpu.PrefetchScalarGridSpec(
            num_scalar_prefetch=1,
            grid=(rows // block,),
            in_specs=specs,
            out_specs=out_specs,
        ),
        out_shape=out_shape,
        compiler_params=PARAMS,
        cost_estimate=cost(4 * rows * depth * len(ks) * hid, rows * (2 * wide + 2 * hid) + 4 * depth * len(ks) * hid),
        name="hidden_rows",
    )(at, *args)


def moment_kernel(at_ref, *refs):
    coef_ref, h0_ref, h1_ref, own_ref, m0_ref, m1_ref, n_ref = refs[-7:]
    lt = rows_of(refs[:-7])
    for which, h_ref, m_ref in ((0, h0_ref, m0_ref), (1, h1_ref, m1_ref)):
        hi, lo = split(mm_split(stacked(lt * coef_ref[which : which + 1, :]), h_ref[...]))
        m_ref[0] = hi
        m_ref[1] = lo
    a_hi, a_lo = split(lt)
    b_hi, b_lo = split(own_ref[...])
    n_ref[...] = mm(a_hi, b_hi, NT) + mm(a_lo, b_hi, NT) + mm(a_hi, b_lo, NT)


def moments(at, lows, coef, h0, h1, lt):
    peers, rank, rows = lows.shape
    hid = h0.shape[1]
    total, block = peers * rank, peers * rank // 2
    terms = pl.BlockSpec((2, block, hid), lambda i, at: (0, i, 0))
    specs = relative_specs(lows, 0)
    return pl.pallas_call(
        moment_kernel,
        grid_spec=pltpu.PrefetchScalarGridSpec(
            num_scalar_prefetch=1,
            grid=(2,),
            in_specs=[*specs, full_spec(coef), full_spec(h0), full_spec(h1), full_spec(lt)],
            out_specs=[terms, terms, pl.BlockSpec((block, rank), lambda i, at: (i, 0))],
        ),
        out_shape=[jax.ShapeDtypeStruct((2, total, hid), BF)] * 2 + [jax.ShapeDtypeStruct((total, rank), F32)],
        compiler_params=PARAMS,
        cost_estimate=cost(8 * total * rows * hid, 4 * total * (rows + 2 * hid) + 4 * rows * hid),
        name="moments",
    )(at, *[lows] * len(specs), coef, h0, h1, lt)


def grad_kernel(ks, at_ref, m0_ref, m1_ref, n_ref, second_ref, *refs):
    m0, m1 = (m_ref[...].reshape(-1, m_ref.shape[2]) for m_ref in (m0_ref, m1_ref))
    n_hi, n_lo = split(n_ref[...])
    outs = refs[2 * len(ks) :]
    for p, k in enumerate(ks):
        d0, d1 = as_matrix(refs[2 * p]), as_matrix(refs[2 * p + 1])
        o_hi, o_lo = split(second_ref[:, columns(at_ref, k, d0.shape[1])])
        g = mm_split(m0, d0) + mm_split(m1, d1)
        outs[0][:, p * d0.shape[1] : (p + 1) * d0.shape[1]] = g + mm(n_hi, o_hi) + mm(n_lo, o_hi) + mm(n_hi, o_lo)


def grad_sums(at, ms, n, downs, second, ks, start, total):
    hid = ms[0].shape[2]
    rank = second.shape[0]
    depth = downs[0][0][0].shape[2]
    block = min(256, total)
    row = lambda width: pl.BlockSpec((block, width), lambda i, *at: (i + start // block, 0))
    terms = pl.BlockSpec((2, block, hid), lambda i, *at: (0, i + start // block, 0))
    args, specs = [*ms, n, second], [terms, terms, row(rank), full_spec(second)]
    for k in ks:
        args += [arr for arr, _ in downs[k]]
        specs += [placed_spec(item) for item in downs[k]]
    return pl.pallas_call(
        functools.partial(grad_kernel, ks),
        grid_spec=pltpu.PrefetchScalarGridSpec(
            num_scalar_prefetch=1,
            grid=(total // block,),
            in_specs=specs,
            out_specs=pl.BlockSpec((block, len(ks) * depth), lambda i, *at: (i, 0)),
        ),
        out_shape=jax.ShapeDtypeStruct((total, len(ks) * depth), F32),
        compiler_params=PARAMS,
        cost_estimate=cost(8 * total * hid * depth * len(ks), 8 * total * hid + 4 * len(ks) * depth * (total + hid)),
        name="grad_sums",
    )(at, *args)


def key_terms(at_ref, sec_refs, d, k):
    where = columns(at_ref, k, d.shape[1]) if k is not None else slice(None)
    sec = jnp.concatenate([ref[0, :, where] for ref in sec_refs], axis=0)
    return mm_split(stacked(sec), d, NT)


def stage_kernel(ks, carry, at_ref, *refs):
    refs = list(refs)
    near_ref, far_ref, key_ref = refs[-3:]
    del refs[-3:]
    downs = refs[-len(ks) :]
    del refs[-len(ks) :]
    second_ref, n_ref, m_ref = refs[-3:]
    del refs[-3:]
    sums = [refs.pop(), refs.pop()][::-1] if carry else None
    side = pl.program_id(0)
    m = m_ref[...].reshape(-1, m_ref.shape[2])
    key = None
    parts = []
    for k, d_ref in zip(ks, downs):
        d = as_matrix(d_ref)
        term = key_terms(at_ref, refs, d, k)
        key = term if key is None else key + term
        g = mm_split(m, d)
        if not carry:
            g += mm_full(n_ref[...], second_ref[:, columns(at_ref, k, d.shape[1])])
        parts.append(g)
    key_ref[...] = key
    for which, out_ref in ((0, near_ref), (1, far_ref)):

        @pl.when(side == which)
        def _():
            for p, g in enumerate(parts):
                where = slice(p * g.shape[1], (p + 1) * g.shape[1])
                out_ref[:, where] = g + sums[which][:, where] if carry else g


def down_stage(at, seconds, second, n, m, downs, ks, sums=()):
    peers, rank, width = seconds.shape
    depth = downs[0][0][0].shape[2]
    hid = downs[0][0][0].shape[1]
    total, block = peers * rank, peers * rank // 2
    row = lambda wide: pl.BlockSpec((block, wide), lambda i, at: (i, 0))
    specs = relative_specs(seconds, 0)
    items = [downs[k][0] for k in ks]
    args = [*[seconds] * len(specs), *sums, second, n, m, *(arr for arr, _ in items)]
    specs += [full_spec(v) for v in sums]
    specs += [full_spec(second), row(rank), pl.BlockSpec((2, block, hid), lambda i, at: (0, i, 0))]
    specs += [placed_spec(item) for item in items]
    part = jax.ShapeDtypeStruct((block, len(ks) * depth), F32)
    near, far, key = pl.pallas_call(
        functools.partial(stage_kernel, ks, len(sums) > 0),
        grid_spec=pltpu.PrefetchScalarGridSpec(
            num_scalar_prefetch=1, grid=(2,), in_specs=specs, out_specs=[full_spec(part), full_spec(part), row(hid)]
        ),
        out_shape=[part, part, jax.ShapeDtypeStruct((total, hid), F32)],
        compiler_params=PARAMS,
        cost_estimate=cost(8 * total * hid * len(ks) * depth, 4 * total * (width + 2 * hid)),
        name="down_stage",
    )(at, *args)
    return (near, far), key


def own_kernel(at_ref, *refs):
    *sec_refs, own_ref, s_ref = refs
    hi, lo = split(rows_of(sec_refs))
    own_hi, own_lo = split(own_ref[...])
    s_ref[...] = mm(hi, own_hi, NT) + mm(lo, own_hi, NT) + mm(hi, own_lo, NT)


def own_products(at, seconds, second):
    peers, rank, width = seconds.shape
    total, block = peers * rank, peers * rank // 2
    specs = relative_specs(seconds, 0)
    return pl.pallas_call(
        own_kernel,
        grid_spec=pltpu.PrefetchScalarGridSpec(
            num_scalar_prefetch=1,
            grid=(2,),
            in_specs=[*specs, full_spec(second)],
            out_specs=pl.BlockSpec((block, rank), lambda i, at: (i, 0)),
        ),
        out_shape=jax.ShapeDtypeStruct((total, rank), F32),
        compiler_params=PARAMS,
        cost_estimate=cost(6 * total * rank * width, 4 * total * width),
        name="own_products",
    )(at, *[seconds] * len(specs), second)


def back_kernel(at_ref, *refs):
    *sec_refs, d0_ref, d1_ref, k0_ref, k1_ref, h0_ref, h1_ref, coef_ref, s_ref, lt_ref, b_ref = refs
    b = None
    for e, d_ref, k_ref, h_ref in ((0, d0_ref, k0_ref, h0_ref), (1, d1_ref, k1_ref, h1_ref)):
        key = k_ref[...] + key_terms(at_ref, sec_refs, as_matrix(d_ref), None)
        term = mm_split(stacked(key), h_ref[...], NT) * coef_ref[e : e + 1, :]
        b = term if b is None else b + term
    b_ref[...] = b + mm_full(s_ref[...], lt_ref[...])


def back_rows(at, seconds, down, last, keys, s, h0, h1, coef, lt, side):
    hid = keys[0].shape[1]
    rows = h0.shape[0]
    rank = s.shape[1]
    block = s.shape[0] // 2
    row = lambda width: pl.BlockSpec((block, width), lambda i, at: (side, 0))
    specs = relative_specs(seconds, side, last, down[0][0].shape[2])
    args = [seconds] * len(specs)
    specs += [*(placed_spec(item) for item in down), row(hid), row(hid)]
    specs += [full_spec(h0), full_spec(h1), full_spec(coef), row(rank), full_spec(lt)]
    return pl.pallas_call(
        back_kernel,
        grid_spec=pltpu.PrefetchScalarGridSpec(
            num_scalar_prefetch=1,
            grid=(1,),
            in_specs=specs,
            out_specs=pl.BlockSpec((block, rows), lambda i, at: (0, 0)),
        ),
        out_shape=jax.ShapeDtypeStruct((block, rows), F32),
        compiler_params=PARAMS,
        cost_estimate=cost(64000 * block * rows * hid, 8000 * block * hid + 4000 * rows * hid + 4000 * block * rows),
        name="back_rows",
    )(at, *args, *(arr for arr, _ in down), *keys, h0, h1, coef, s, lt)


def swap(v, axis, mask):
    size = lax.axis_size(axis)
    return lax.ppermute(v, axis, [(i, i ^ mask) for i in range(size)])


def after(v, *done):
    return lax.optimization_barrier((v, *done))[0] if done else v


def spread(own, orders, wait=(), passing=()):
    size = lax.axis_size("dp")
    got = [[(own, p) for p in range(len(orders))]]
    for k in range(1, size):
        if k & (k - 1) == 0:
            sent = swap(after(own, *wait), "dp", k)
            got.append([(sent, p) for p in range(len(orders))])
            continue
        items = []
        for p, highest_last in enumerate(orders):
            bit = 1 << (k.bit_length() - 1) if highest_last else k & -k
            arr, place = got[k ^ bit][p]
            items.append((swap(after(arr[place : place + 1], *passing), "dp", bit), 0))
        got.append(items)
    return got


def chip_blocks(v, waits):
    got = [v]
    for m in range(1, lax.axis_size("expert") // 2):
        bit = m & -m if m & 1 else m
        got.append(swap(after(got[m ^ bit], *waits.get(m, ())), "expert", 2 * bit))
    return got


def both_cores(blocks):
    mine = jnp.stack(blocks)
    return mine, swap(mine, "expert", 1)


def chip_sums(near, far):
    got = swap(far, "expert", 1)
    half = near.shape[0] // 2
    return near[:half] + got[:half], near[half:] + got[half:]


def sum_over_chips(keep, send, dtype, waits=()):
    mask, first = 2, None
    while True:
        wait, *waits = waits or ((),)
        total = keep + swap(after(send.astype(dtype), *wait), "expert", mask).astype(F32)
        first = total if first is None else first
        half = total.shape[0] // 2
        if half == 0:
            return total[0], first
        keep, send = total[:half], total[half:]
        mask *= 2


def shards(
    tokens,
    initial_expert_index,
    pruned_expert_index,
    initial_router_scores,
    pruned_router_scores,
    gate_weight,
    up_weight,
    down_weight,
    adapter_first_weight,
    adapter_second_weight,
):
    peers = lax.axis_size("expert")
    groups = lax.axis_size("dp")
    place = lax.axis_index("dp")
    me = lax.axis_index("expert")
    chips = peers // 2
    tok, width = tokens.shape
    hid = gate_weight.shape[2]
    depth = gate_weight.shape[1]
    rank = adapter_first_weight.shape[2]

    chosen = table_columns(peers)
    kind = jnp.arange(8, dtype=jnp.int32)[:, None]
    column = jnp.arange(chosen.shape[1], dtype=jnp.int32)[None, :]
    pick = ((column % (3 * peers) == 3 * me + kind) & (kind < 3) & (column < 9 * peers)).astype(BF)
    at = jnp.stack([me // 2, me % 2, place, me]).astype(jnp.int32)
    first_t = jnp.concatenate(split(adapter_first_weight[0].T), axis=0)
    second = adapter_second_weight[0]

    last = groups - 1
    most = list(range(last))
    def direct(got):
        return [got[1 << p][0][0] for p in range(groups.bit_length() - 1)]

    def ends(got):
        return [arr for arr, _ in got[last]]

    def both(first, second):
        return [a + b for a, b in zip(first, second)]

    packet = packets(
        tokens, initial_expert_index, pruned_expert_index, initial_router_scores, pruned_router_scores, chosen
    )
    own_gate0, own_up0 = gate_weight[0:1], up_weight[0:1]
    own_gate1, own_up1, own_down0, own_down1 = own_slices(
        (gate_weight, 1), (up_weight, 1), (down_weight, 0), (down_weight, 1)
    )
    gate0 = spread(own_gate0, (True,))
    up0 = spread(own_up0, (False,))
    w0 = both(gate0, up0)
    x = lax.all_gather(packet, "expert", axis=0, tiled=True)
    seconds = lax.all_gather(after(second, *direct(gate0), *direct(up0), own_gate1), "expert", axis=0)
    h0, lt, coef = hidden_rows(at, x, w0, most + [last], (), True, first_t, pick)

    gate1 = spread(own_gate1, (True,), direct(up0))
    up1 = spread(own_up1, (False,), ends(gate0) + ends(up0))
    w1 = both(gate1, up1)
    direct1 = direct(gate1) + direct(up1)
    lows = lax.all_gather(after(lt, *direct1), "expert", axis=0)
    s = own_products(at, seconds, second)
    (h1,) = hidden_rows(at, after(x, s), w1, most + [last])
    down0 = spread(own_down0, (True,), (*ends(gate1), *ends(up1), s))
    *ms, n = moments(at, lows, coef, h0, h1, lt)
    parts, key0 = down_stage(at, seconds, second, n, ms[0], down0, most)
    down1 = spread(own_down1, (False,), (h1,), (key0,))

    def blocks(v):
        return v.reshape(chips, rank, -1)

    parts, key1 = down_stage(at, seconds, second, n, ms[1], down1, most, parts)
    downs = both(down0, down1)

    def back(side, *wait):
        return blocks(back_rows(at, seconds, downs[last], last, (key0, key1), s, h0, h1, after(coef, *wait), lt, side))

    far = back(1)
    far = back(1)
    near_early, far_early = (blocks(part) for part in parts)
    early = chip_sums(near_early, far_early)
    near = back(0, far, early[1])
    sums = chip_sums(near, far)
    early, early_first = sum_over_chips(*early, BF)
    late = chip_sums(
        *(
            blocks(grad_sums(at, [after(ms[0], sums[1]), ms[1]], n, downs, second, [last], start, chips * rank))
            for start in (0, chips * rank)
        )
    )
    late, late_first = sum_over_chips(*late, BF, ((early_first,),))
    b, b_first = sum_over_chips(*sums, BF, ((), (late_first,)))
    b = b * coef[2:3, :]

    over_tokens = (((0,), (1,)), ((), ()))
    b_hi, b_lo = split(b)
    part_a = mm(h0, b_hi, over_tokens) + mm(h0, b_lo, over_tokens)
    rows = hid // groups
    grad_a = lax.dynamic_slice_in_dim(part_a, place * rows, rows, 0)
    for k in range(1, groups):
        grad_a = grad_a + swap(lax.dynamic_slice_in_dim(part_a, (place ^ k) * rows, rows, 0), "dp", k)
    grad_b = early[:, :depth]
    for k in range(1, groups):
        part = late if k == last else early[:, k * depth : (k + 1) * depth]
        grad_b = grad_b + swap(after(part, b_first), "dp", k)
    return grad_a[None], grad_b[None]


def solution(mesh):
    placed = (
        P(("dp", "expert"), None),
        P(("dp", "expert"), None),
        P(("dp", "expert"), None),
        P(("dp", "expert"), None),
        P(("dp", "expert"), None),
        P("expert", "dp", None),
        P("expert", "dp", None),
        P("expert", None, "dp"),
        P("expert", None, None),
        P("expert", None, None),
    )
    return jax.shard_map(
        shards,
        mesh=mesh,
        in_specs=placed,
        out_specs=(P("expert", "dp", None), P("expert", None, "dp")),
        check_vma=False,
    )
```
